256 devices in a mesh: dp: 32 (over y, x, core), mp: 8 (over z).
Axes of the slice: x: 4, y: 4, z: 8, core: 2. Of those that a mesh axis runs over, the one named last changes fastest.
Arguments:
- x_in: bfloat16 [16384, 2304], P(('dp', 'mp')), may hold values from -6 to 6
- out_grad: bfloat16 [16384, 2304], P(('dp', 'mp')), may hold values from -0.0625 to 0.0625
- context: bfloat16 [16384, 2048], P('dp', 'mp'), may hold values from -6 to 6
- query_grad: bfloat16 [16384, 2048], P('dp', 'mp'), may hold values from -0.0625 to 0.0625
- keyval_grad: bfloat16 [2, 16384, 1024], P(None, 'dp', 'mp'), may hold values from -0.0625 to 0.0625
- query_weight: bfloat16 [2304, 2048], P(None, 'mp'), may hold values from -2 to 2
- keyval_weight: bfloat16 [2, 2304, 1024], P(None, None, 'mp'), may hold values from -2 to 2
- wide_error: bfloat16 [32, 2, 2304, 2048], P('dp', None, None, 'mp'), may hold values from -1.1953125 to 1.1953125
- narrow_error: bfloat16 [32, 2, 2304, 1024], P('dp', None, None, 'mp'), may hold values from -1.1953125 to 1.1953125
- wide_start: float32 [2, 2048, 32], P(None, 'mp'), may hold values from -6 to 6
- narrow_start: float32 [2, 1024, 32], P(None, 'mp'), may hold values from -6 to 6
Outputs:
- input_grad: bfloat16 [16384, 2304], P(('dp', 'mp'))
- wide_p: float32 [2, 8, 2304, 32], P(None, 'mp', 'dp')
- narrow_p: float32 [2, 8, 2304, 32], P(None, 'mp', 'dp')
- wide_q: float32 [2, 2048, 32], P(None, 'mp')
- narrow_q: float32 [2, 1024, 32], P(None, 'mp')
- wide_error_new: bfloat16 [32, 2, 2304, 2048], P('dp', None, None, 'mp')
- narrow_error_new: bfloat16 [32, 2, 2304, 1024], P('dp', None, None, 'mp')
The draws below stay inside these ranges and needn't reach their ends.
All inputs are finite; a program needn't handle non-finite values.
Results may differ from the reference program's by a relative error of at most 0.0016.
Values may be sent and summed in bfloat16 or wider, within the bound.
A program may use at most 128 MiB of HBM per device.

```python
import jax
import jax.numpy as jnp
from jax import lax

D = 2304
QH = 16
KVH = 8
HD = 128
RANK = 32
TOK = 512
QW = 2048
KW = 1024
REPLICAS = 32
TOKENS = 16384
N_DP = 32
N_MP = 8


def steps_of(rng, shape, pieces, smallest, largest):
    def one(dim, parts):
        steps = jax.random.uniform(jax.random.fold_in(jax.random.fold_in(rng, 6), dim), (parts,), jnp.float32, smallest / len(pieces), largest / len(pieces))
        return jnp.repeat(jnp.exp(steps), shape[dim] // parts).reshape((-1,) + (1,) * (len(shape) - dim - 1))

    factor_of = one(*pieces[0])
    for cut in pieces[1:]:
        factor_of = factor_of * one(*cut)
    return factor_of


def centred(own_key, dims, deviation, bound, pieces=(), held_as=jnp.bfloat16):
    factor_of = steps_of(own_key, dims, pieces, -0.22, 0.18) if pieces else 1.0
    values = jax.random.normal(own_key, dims, jnp.float32) * deviation * factor_of
    return jnp.minimum(jnp.maximum(values, -bound), bound).astype(held_as)


def setup_inputs(seed: int = 0) -> dict:
    keys = jax.random.split(jax.random.key(seed), 12)
    return {
        "x_in": centred(keys[0], (TOKENS, D), 1.0, 6.0, ((0, 256),)),
        "out_grad": centred(keys[1], (TOKENS, D), (16 * TOK) ** -0.5, 0.0625, ((0, 256),)),
        "context": centred(keys[2], (TOKENS, QW), 1.0, 6.0, ((0, 32), (1, 8))),
        "query_grad": centred(keys[3], (TOKENS, QW), (16 * TOK) ** -0.5, 0.0625, ((0, 32), (1, 8))),
        "keyval_grad": centred(keys[4], (2, TOKENS, KW), (16 * TOK) ** -0.5, 0.0625, ((1, 32), (2, 8))),
        "query_weight": centred(keys[5], (D, QW), ((QH + 2 * KVH) * HD // TOK) ** -0.5, 2.0, ((1, 8),)),
        "keyval_weight": centred(keys[6], (2, D, KW), ((QH + 2 * KVH) * HD // TOK) ** -0.5, 2.0, ((2, 8),)),
        "wide_error": centred(keys[7], (REPLICAS, 2, D, QW), 0.2, 1.1953125, ((0, 32), (3, 8))),
        "narrow_error": centred(keys[8], (REPLICAS, 2, D, KW), 0.2, 1.1953125, ((0, 32), (3, 8))),
        "wide_start": centred(keys[9], (2, QW, RANK), 1.0, 6.0, ((1, 8),), jnp.float32),
        "narrow_start": centred(keys[10], (2, KW, RANK), 1.0, 6.0, ((1, 8),), jnp.float32),
    }


HIGH = lax.Precision.HIGHEST

def columns(factor):
    rank_size = factor.shape[2]
    col_order = jnp.arange(rank_size, dtype=jnp.int32)

    def advance(column_at, current):
        column_at = column_at.astype(jnp.int32)
        column = lax.dynamic_slice_in_dim(current, column_at, 1, 2)
        column = column / jnp.sqrt(lax.optimization_barrier(jnp.sum(column * column, axis=1, keepdims=True)))
        projected = lax.optimization_barrier(jnp.sum(column * current, axis=1, keepdims=True))
        current = current - column * jnp.where(col_order > column_at, projected, jnp.zeros_like(projected))
        return lax.dynamic_update_slice_in_dim(current, column, column_at, 2)
    return lax.fori_loop(jnp.int32(0), jnp.int32(rank_size), advance, factor)

def reference(x_in, out_grad, context, query_grad, keyval_grad, query_weight, keyval_weight, wide_error, narrow_error, wide_start, narrow_start):
    input_grad = (jnp.dot(query_grad, query_weight.T, preferred_element_type=jnp.float32) + jnp.dot(keyval_grad[0], keyval_weight[0].T, preferred_element_type=jnp.float32) + jnp.dot(keyval_grad[1], keyval_weight[1].T, preferred_element_type=jnp.float32)).astype(jnp.bfloat16)
    inputs = x_in.reshape(N_DP, TOK, D)
    outputs = out_grad.reshape(N_DP, TOK, D)
    contexts = context.reshape(N_DP, TOK, QW)
    queries = query_grad.reshape(N_DP, TOK, QW)
    keyvals = keyval_grad.reshape(2, N_DP, TOK, KW)
    query_block = QW // N_MP
    keyval_block = KW // N_MP
    wide_blocks = wide_start.reshape(2, N_MP, query_block, RANK)
    narrow_blocks = narrow_start.reshape(2, N_MP, keyval_block, RANK)

    def sums(seq_index):
        x_rows = inputs[seq_index]
        wide_sum = jnp.stack([jnp.dot(x_rows.T, queries[seq_index], preferred_element_type=jnp.float32), jnp.dot(outputs[seq_index].T, contexts[seq_index], preferred_element_type=jnp.float32)])
        wide_sum = wide_sum + wide_error[seq_index].astype(jnp.float32)
        narrow_sum = jnp.stack([jnp.dot(x_rows.T, keyvals[0, seq_index], preferred_element_type=jnp.float32), jnp.dot(x_rows.T, keyvals[1, seq_index], preferred_element_type=jnp.float32)])
        narrow_sum = narrow_sum + narrow_error[seq_index].astype(jnp.float32)
        return (wide_sum.reshape(2, D, N_MP, query_block), narrow_sum.reshape(2, D, N_MP, keyval_block))
    seq_ids = jnp.arange(N_DP, dtype=jnp.int32)

    def add_factor(running, seq_index):
        wide_sum, narrow_sum = sums(seq_index)
        wide_part = jnp.einsum('bdmc,bmcr->bmdr', wide_sum, wide_blocks, precision=HIGH)
        narrow_part = jnp.einsum('bdmc,bmcr->bmdr', narrow_sum, narrow_blocks, precision=HIGH)
        return ((running[0] + wide_part, running[1] + narrow_part), None)
    empty = jnp.zeros((2, N_MP, D, RANK), jnp.float32)
    (wide_factor, narrow_factor), unused = lax.scan(add_factor, (empty, empty), seq_ids)
    stacked = jnp.concatenate([wide_factor, narrow_factor], axis=0).reshape(4 * N_MP, D, RANK)
    factor_hat = columns(stacked).reshape(4, N_MP, D, RANK)
    wide_p = factor_hat[:2]
    narrow_p = factor_hat[2:]

    def add_back(running, seq_index):
        wide_sum, narrow_sum = sums(seq_index)
        wide_part = jnp.einsum('bdmc,bmdr->bmcr', wide_sum, wide_p, precision=HIGH)
        narrow_part = jnp.einsum('bdmc,bmdr->bmcr', narrow_sum, narrow_p, precision=HIGH)
        return ((running[0] + wide_part, running[1] + narrow_part), None)
    start_back = (jnp.zeros((2, N_MP, query_block, RANK), jnp.float32), jnp.zeros((2, N_MP, keyval_block, RANK), jnp.float32))
    (wide_back, narrow_back), unused = lax.scan(add_back, start_back, seq_ids)
    wide_back = wide_back / jnp.float32(N_DP)
    narrow_back = narrow_back / jnp.float32(N_DP)

    def new_error(seq_index):
        wide_sum, narrow_sum = sums(seq_index)
        wide_new = wide_sum - jnp.einsum('bmdr,bmcr->bdmc', wide_p, wide_back, precision=HIGH)
        narrow_new = narrow_sum - jnp.einsum('bmdr,bmcr->bdmc', narrow_p, narrow_back, precision=HIGH)
        return (wide_new.reshape(2, D, QW).astype(jnp.bfloat16), narrow_new.reshape(2, D, KW).astype(jnp.bfloat16))
    wide_error_new, narrow_error_new = lax.map(new_error, seq_ids)
    wide_q = wide_back.reshape(2, QW, RANK)
    narrow_q = narrow_back.reshape(2, KW, RANK)
    return (input_grad, wide_p, narrow_p, wide_q, narrow_q, wide_error_new, narrow_error_new)
```

```python
import jax
import jax.numpy as jnp
from jax import lax
from jax.experimental import pallas as pl
from jax.experimental.pallas import tpu as pltpu
from jax.sharding import PartitionSpec as P

MESH = pl.DeviceIdType.MESH
F32 = jnp.float32
BF16 = jnp.bfloat16

D = 2304
HALF = D // 2
TOK = 512
SHARE = 64
PART = SHARE // 2
RANK = 32
N_DP = 32
N_MP = 8
CHIPS = N_DP // 2
ROWS_P = D // N_DP
COLS = ((0, 256), (256, 128), (384, 128), (512, 256))
INTO = 512
ALL = 768


def split(value):
    high = value.astype(BF16)
    return high, (value - high.astype(F32)).astype(BF16)


def dot(a, b, on_a=1, on_b=0):
    return lax.dot_general(a, b, (((on_a,), (on_b,)), ((), ())), preferred_element_type=F32)


def kernel(
    x_in, out_grad, context, query_grad, keyval_grad, query_weight, keyval_weight,
    wide_error, narrow_error, wide_start, narrow_start,
    input_grad, wide_p, narrow_p, wide_q, narrow_q, wide_new, narrow_new,
    xf, yf, gv, wv, ev, sw, sn, st, tx, ty, pg, rr, sh, sl,
    fl, ra, rb, ff, rowbuf, pb, pt, pc, ql, rq, qf, qbd, nv, ig, pst, qsw, qsn,
    load_sem, x_send, x_recv, y_send, y_recv, z_send, z_recv,
    a_send, a_recv, b_send, b_recv, c_send, c_recv, d_send, d_recv,
    e_send, e_recv, f_send, f_recv, out_sem, small_sem,
):
    dp = lax.axis_index("dp")
    mp = lax.axis_index("mp")
    core = dp % 2
    chip = dp // 2
    mate = dp + 1 - 2 * core
    ring = ((mp + 1) % N_MP, (mp + N_MP - 1) % N_MP)

    def along(way, steps):
        return (mp + steps) % N_MP if way == 0 else (mp + N_MP - steps) % N_MP

    loads = [
        (query_grad, gv.at[:, 0:256]),
        (keyval_grad.at[0], gv.at[:, 256:384]),
        (keyval_grad.at[1], gv.at[:, 384:512]),
        (query_weight, wv.at[:, 0:256]),
        (keyval_weight.at[0], wv.at[:, 256:384]),
        (keyval_weight.at[1], wv.at[:, 384:512]),
        (wide_start, sw),
        (narrow_start, sn),
        (wide_error.at[0, 0], ev.at[:, 0:256]),
        (narrow_error.at[0, 0], ev.at[:, 256:384]),
        (narrow_error.at[0, 1], ev.at[:, 384:512]),
        (wide_error.at[0, 1], ev.at[:, 512:768]),
        (context, gv.at[:, 512:768]),
        (x_in, xf.at[pl.ds(pl.multiple_of(mp * SHARE, SHARE), SHARE), :]),
        (out_grad, yf.at[pl.ds(pl.multiple_of(mp * SHARE, SHARE), SHARE), :]),
    ]
    loads = [pltpu.make_async_copy(a, b, load_sem.at[i]) for i, (a, b) in enumerate(loads)]
    for copy in loads:
        copy.start()

    barrier = pltpu.get_barrier_semaphore()
    for way in (0, 1):
        pl.semaphore_signal(barrier, inc=1, device_id=(dp, ring[way]), device_id_type=MESH)

    @pl.loop(1, N_DP)
    def _(k):
        pl.semaphore_signal(barrier, inc=1, device_id=((dp + k) % N_DP, mp), device_id_type=MESH)

    pl.semaphore_wait(barrier, N_DP + 1)

    def hop(own, full, send, recv, way, step, role):
        part = way if role == 0 else 1 - way
        owner = along(1 - way, step - 1)
        rows = pl.ds(pl.multiple_of(owner * SHARE + part * PART, PART), PART)
        src = own.at[part * PART:(part + 1) * PART, :] if step == 1 else full.at[rows, :]
        return pltpu.make_async_remote_copy(
            src_ref=src, dst_ref=full.at[rows, :],
            send_sem=send.at[way, step - 1, role], recv_sem=recv.at[way, step - 1, role],
            device_id=(dp, ring[way]), device_id_type=MESH,
        )

    def x_hop(way, step, role):
        return hop(x_in, xf, x_send, x_recv, way, step, role)

    def y_hop(way, step, role):
        return hop(out_grad, yf, y_send, y_recv, way, step, role)

    def first(make):
        for role in (0, 1):
            for way in (0, 1):
                make(way, 1, role).start()

    def forward(make, step, role):
        for way in (0, 1):
            make(way, step - 1, role).wait_recv()
            make(way, step, role).start()

    def finish_ring(make):
        for way in (0, 1):
            make(way, 3, 1).wait_recv()
            make(way, 4, 0).wait_recv()

    def drain_ring(make):
        for way in (0, 1):
            for step in (1, 2, 3, 4):
                for role in (0, 1):
                    if (step, role) != (4, 1):
                        make(way, step, role).wait_send()

    def z_hop(way, step, role):
        part = way if role == 0 else 1 - way
        dest = along(way, 5 - step)
        rows = pl.ds(pl.multiple_of(dest * SHARE + part * PART, PART), PART)
        here = slice(part * PART, (part + 1) * PART)
        if step == (1 if role == 0 else 2):
            src = pg.at[rows, :]
        else:
            src = rr.at[way, step - 2, here, :]
        return pltpu.make_async_remote_copy(
            src_ref=src, dst_ref=rr.at[way, step - 1, here, :],
            send_sem=z_send.at[way, step - 1, role], recv_sem=z_recv.at[way, step - 1, role],
            device_id=(dp, ring[way]), device_id_type=MESH,
        ), rows, here

    def z_first():
        for way in (0, 1):
            z_hop(way, 1, 0)[0].start()
        for way in (0, 1):
            z_hop(way, 2, 1)[0].start()

    def z_step(step, role):
        for way in (0, 1):
            z_hop(way, step - 1, role)[0].wait_recv()
            copy, rows, here = z_hop(way, step, role)
            rr[way, step - 2, here, :] += pg[rows, :]
            copy.start()

    first(x_hop)
    for i in range(6):
        loads[i].wait()

    @pl.loop(0, 9)
    def _(j):
        cols = pl.ds(pl.multiple_of(j * 256, 256), 256)
        pg[:, cols] = dot(gv[:, 0:INTO], wv[cols, :], 1, 1)

    forward(x_hop, 2, 0)
    forward(x_hop, 2, 1)

    for i in (6, 7):
        loads[i].wait()
    for b, (at, width) in enumerate(COLS):
        start = sw[0 if b == 0 else 1] if width == 256 else sn[b - 1]
        high, low = split(jnp.transpose(start))
        st[0:RANK, at:at + width] = high
        st[RANK:2 * RANK, at:at + width] = low
    loads[12].wait()
    for b, (at, width) in enumerate(COLS):
        t = dot(st[:, at:at + width], gv[:, at:at + width], 1, 1)
        high, low = split(t[:RANK] + t[RANK:])
        if b < 3:
            tx[b * RANK:(b + 1) * RANK, :] = high
            tx[96 + b * RANK:96 + (b + 1) * RANK, :] = low
        else:
            ty[0:RANK, :] = high
            ty[RANK:2 * RANK, :] = low
    qbd[...] = jnp.zeros_like(qbd)
    ql[:, ALL:] = jnp.zeros((RANK, 1024 - ALL), F32)

    forward(x_hop, 3, 0)
    forward(x_hop, 3, 1)

    for i in (8, 9, 10, 11):
        loads[i].wait()

    @pl.loop(0, 6)
    def _(j):
        rows = pl.ds(pl.multiple_of(j * 384, 384), 384)
        lanes = pl.ds(pl.multiple_of((j % 3) * 384, 384), 384)
        for b, (at, width) in enumerate(COLS):
            e = dot(st[:, at:at + width], ev[rows, at:at + width], 1, 1)
            fl[j // 3, b * RANK:(b + 1) * RANK, lanes] = e[:RANK] + e[RANK:]

    forward(x_hop, 4, 0)
    first(y_hop)
    loads[13].wait()
    finish_ring(x_hop)

    @pl.loop(0, 6)
    def _(j):
        cols = pl.ds(pl.multiple_of(j * 384, 384), 384)
        lanes = pl.ds(pl.multiple_of((j % 3) * 384, 384), 384)
        f = dot(tx[...], xf[:, cols])
        fl[j // 3, 0:96, lanes] += f[:96] + f[96:]

    forward(y_hop, 2, 0)
    forward(y_hop, 2, 1)

    @pl.loop(0, 9)
    def _(j):
        rows = pl.ds(pl.multiple_of(j * 256, 256), 256)
        total = dot(xf[:, rows], gv[:, 0:INTO], 0, 0) + ev[rows, 0:INTO].astype(F32)
        high, low = split(total)
        sh[rows, 0:INTO] = high
        sl[rows, 0:INTO] = low

    forward(y_hop, 3, 0)
    forward(y_hop, 3, 1)
    forward(y_hop, 4, 0)
    z_first()
    loads[14].wait()
    finish_ring(y_hop)

    @pl.loop(0, 6)
    def _(j):
        cols = pl.ds(pl.multiple_of(j * 384, 384), 384)
        lanes = pl.ds(pl.multiple_of((j % 3) * 384, 384), 384)
        f = dot(ty[...], yf[:, cols])
        fl[j // 3, 96:128, lanes] += f[:RANK] + f[RANK:]

    a_copy = pltpu.make_async_remote_copy(
        src_ref=fl.at[1 - core], dst_ref=ra, send_sem=a_send, recv_sem=a_recv,
        device_id=(mate, mp), device_id_type=MESH,
    )
    a_copy.start()

    @pl.loop(0, 9)
    def _(j):
        rows = pl.ds(pl.multiple_of(j * 256, 256), 256)
        total = dot(yf[:, rows], gv[:, INTO:ALL], 0, 0) + ev[rows, INTO:ALL].astype(F32)
        high, low = split(total)
        sh[rows, INTO:ALL] = high
        sl[rows, INTO:ALL] = low

    a_copy.wait_recv()
    fl[core] += ra[...]

    def b_copy(k):
        other = (chip + k) % CHIPS
        return pltpu.make_async_remote_copy(
            src_ref=fl.at[core, pl.ds(pl.multiple_of(other * 8, 8), 8), :], dst_ref=rb.at[k - 1],
            send_sem=b_send.at[k - 1], recv_sem=b_recv.at[k - 1],
            device_id=(2 * other + core, mp), device_id_type=MESH,
        )

    own_rows = pl.ds(pl.multiple_of(chip * 8, 8), 8)

    def c_copy(k):
        other = (chip + k) % CHIPS
        own = ff.at[core, own_rows, :]
        return pltpu.make_async_remote_copy(
            src_ref=own, dst_ref=own,
            send_sem=c_send.at[k - 1], recv_sem=c_recv.at[k - 1],
            device_id=(2 * other + core, mp), device_id_type=MESH,
        )

    @pl.loop(1, CHIPS)
    def _(k):
        b_copy(k).start()

    z_step(2, 0)

    @pl.loop(1, CHIPS)
    def _(k):
        b_copy(k).wait_recv()

    ff[core, own_rows, :] = fl[core, own_rows, :] + jnp.sum(rb[...], axis=0)

    @pl.loop(1, CHIPS)
    def _(k):
        c_copy(k).start()

    z_step(3, 1)

    @pl.loop(1, CHIPS)
    def _(k):
        c_copy(k).wait_recv()

    d_copy = pltpu.make_async_remote_copy(
        src_ref=ff.at[core], dst_ref=ff.at[core], send_sem=d_send, recv_sem=d_recv,
        device_id=(mate, mp), device_id_type=MESH,
    )
    d_copy.start()
    z_step(3, 0)
    a_copy.wait_send()

    @pl.loop(1, CHIPS)
    def _(k):
        b_copy(k).wait_send()
        c_copy(k).wait_send()

    d_copy.wait()

    def gram_schmidt(block):
        @pl.loop(0, 8)
        def _(i):
            norms = []
            for b in range(4):
                row = [ff[h, pl.ds(b * RANK + block * 8 + i, 1), :] for h in (0, 1)]
                for h in (0, 1):
                    rowbuf[h, b * 8:b * 8 + 8, :] = jnp.broadcast_to(row[h], (8, HALF))
                norms.append(jnp.sum(row[0] * row[0] + row[1] * row[1], axis=1, keepdims=True))
            later = lax.broadcasted_iota(jnp.int32, (8, 1), 0) > i
            scales = {}
            for b in range(4):
                for t in range(block, 4):
                    at = slice(b * RANK + t * 8, b * RANK + t * 8 + 8)
                    r = slice(b * 8, b * 8 + 8)
                    dots = jnp.sum(
                        ff[0, at, :] * rowbuf[0, r, :] + ff[1, at, :] * rowbuf[1, r, :],
                        axis=1, keepdims=True,
                    )
                    scale = dots / norms[b]
                    scales[b, t] = jnp.where(later, scale, 0.0) if t == block else scale
            for b in range(4):
                for t in range(block, 4):
                    at = slice(b * RANK + t * 8, b * RANK + t * 8 + 8)
                    for h in (0, 1):
                        ff[h, at, :] -= scales[b, t] * rowbuf[h, b * 8:b * 8 + 8, :]

    gram_schmidt(0)
    gram_schmidt(1)
    z_step(4, 1)
    gram_schmidt(2)
    gram_schmidt(3)
    for b in range(4):
        at = slice(b * RANK, (b + 1) * RANK)
        squares = jnp.sum(ff[0, at, :] * ff[0, at, :] + ff[1, at, :] * ff[1, at, :], axis=1, keepdims=True)
        size = jnp.sqrt(squares)
        for h in (0, 1):
            unit = ff[h, at, :] / size
            ff[h, at, :] = unit
            high, low = split(unit)
            pb[2 * b * RANK:(2 * b + 1) * RANK, h * HALF:(h + 1) * HALF] = high
            pb[(2 * b + 1) * RANK:(2 * b + 2) * RANK, h * HALF:(h + 1) * HALF] = low

    for b, (at, width) in enumerate(COLS):
        both = dot(pb[2 * b * RANK:(2 * b + 2) * RANK, :], sh[:, at:at + width])
        rest = dot(pb[2 * b * RANK:(2 * b + 1) * RANK, :], sl[:, at:at + width])
        ql[:, at:at + width] = both[:RANK] + both[RANK:] + rest

    def tile_of(j):
        return (
            pl.ds(pl.multiple_of((j % 4) * 8, 8), 8),
            pl.ds(pl.multiple_of((j // 4) * 128, 128), 128),
        )

    own_tile = tile_of(dp)

    def e_copy(k):
        other = (dp + k) % N_DP
        tile = tile_of(other)
        return pltpu.make_async_remote_copy(
            src_ref=ql.at[tile[0], tile[1]], dst_ref=rq.at[k - 1],
            send_sem=e_send.at[k - 1], recv_sem=e_recv.at[k - 1],
            device_id=(other, mp), device_id_type=MESH,
        )

    def f_copy(k):
        own = qf.at[own_tile[0], own_tile[1]]
        return pltpu.make_async_remote_copy(
            src_ref=own, dst_ref=own,
            send_sem=f_send.at[k - 1], recv_sem=f_recv.at[k - 1],
            device_id=((dp + k) % N_DP, mp), device_id_type=MESH,
        )

    @pl.loop(1, N_DP)
    def _(k):
        e_copy(k).start()

    z_step(4, 0)

    @pl.loop(1, N_DP)
    def _(k):
        e_copy(k).wait_recv()

    qf[own_tile[0], own_tile[1]] = (
        ql[own_tile[0], own_tile[1]] + jnp.sum(rq[...], axis=0)
    ) * (1.0 / N_DP)

    @pl.loop(1, N_DP)
    def _(k):
        f_copy(k).start()

    for h in (0, 1):
        @pl.loop(0, 3)
        def _(j):
            lanes = pl.ds(pl.multiple_of(j * 384, 384), 384)
            rows = pl.ds(pl.multiple_of(h * HALF + j * 384, 384), 384)
            by_row = jnp.transpose(ff[h, :, lanes])
            pt[rows, :] = by_row
            high, low = split(by_row)
            pc[rows, 0:128] = high
            pc[rows, 128:256] = high
            pc[rows, 256:384] = low

    mine = pt[pl.ds(pl.multiple_of(dp * ROWS_P, 8), ROWS_P), :]
    for b in range(4):
        pst[b] = mine[:, b * RANK:(b + 1) * RANK]
    small = [
        pltpu.make_async_copy(pst.at[b], dst, small_sem.at[b])
        for b, dst in enumerate((wide_p.at[0, 0], narrow_p.at[0, 0], narrow_p.at[1, 0], wide_p.at[1, 0]))
    ]
    for copy in small:
        copy.start()

    @pl.loop(1, N_DP)
    def _(k):
        f_copy(k).wait_recv()

    for b, (at, width) in enumerate(COLS):
        q = qf[:, at:at + width]
        high, low = split(q)
        qbd[b * RANK:(b + 1) * RANK, at:at + width] = high
        qbd[128 + b * RANK:128 + (b + 1) * RANK, at:at + width] = low
        qbd[256 + b * RANK:256 + (b + 1) * RANK, at:at + width] = high

    def out_copies(j):
        rows = pl.ds(pl.multiple_of(j * 256, 256), 256)
        targets = (wide_new.at[0, 0], narrow_new.at[0, 0], narrow_new.at[0, 1], wide_new.at[0, 1])
        return [
            pltpu.make_async_copy(nv.at[rows, at:at + width], targets[b].at[rows, :], out_sem.at[j, b])
            for b, (at, width) in enumerate(COLS)
        ]

    @pl.loop(0, 9)
    def _(j):
        rows = pl.ds(pl.multiple_of(j * 256, 256), 256)
        low_rank = dot(pc[rows, :], qbd[...])
        nv[rows, :] = (sh[rows, :].astype(F32) + sl[rows, :].astype(F32) - low_rank).astype(BF16)
        for copy in out_copies(j):
            copy.start()

    for b, (at, width) in enumerate(COLS):
        by_row = jnp.transpose(qf[:, at:at + width])
        if width == 256:
            qsw[0 if b == 0 else 1] = by_row
        else:
            qsn[b - 1] = by_row
    tail = [
        pltpu.make_async_copy(qsw, wide_q, small_sem.at[4]),
        pltpu.make_async_copy(qsn, narrow_q, small_sem.at[5]),
    ]
    for copy in tail:
        copy.start()

    for way in (0, 1):
        for role in (0, 1):
            z_hop(way, 4, role)[0].wait_recv()
    own = pl.ds(pl.multiple_of(mp * SHARE, SHARE), SHARE)
    ig[...] = (pg[own, :] + rr[0, 3] + rr[1, 3]).astype(BF16)
    last = pltpu.make_async_copy(ig, input_grad, small_sem.at[6])
    last.start()

    drain_ring(x_hop)
    drain_ring(y_hop)
    for way in (0, 1):
        for step in (1, 2, 3, 4):
            for role in (0, 1):
                if (step, role) != (1, 1):
                    z_hop(way, step, role)[0].wait_send()

    @pl.loop(1, N_DP)
    def _(k):
        e_copy(k).wait_send()
        f_copy(k).wait_send()

    for copy in small + tail:
        copy.wait()

    @pl.loop(0, 9)
    def _(j):
        for copy in out_copies(j):
            copy.wait()

    last.wait()


def on_device(*args):
    sems = pltpu.SemaphoreType.DMA
    vmem = pltpu.VMEM
    return pl.pallas_call(
        kernel,
        out_shape=(
            jax.ShapeDtypeStruct((SHARE, D), BF16),
            jax.ShapeDtypeStruct((2, 1, ROWS_P, RANK), F32),
            jax.ShapeDtypeStruct((2, 1, ROWS_P, RANK), F32),
            jax.ShapeDtypeStruct((2, 256, RANK), F32),
            jax.ShapeDtypeStruct((2, 128, RANK), F32),
            jax.ShapeDtypeStruct((1, 2, D, 256), BF16),
            jax.ShapeDtypeStruct((1, 2, D, 128), BF16),
        ),
        in_specs=[pl.BlockSpec(memory_space=pl.ANY)] * 11,
        out_specs=tuple([pl.BlockSpec(memory_space=pl.ANY)] * 7),
        scratch_shapes=[
            vmem((TOK, D), BF16),
            vmem((TOK, D), BF16),
            vmem((TOK, ALL), BF16),
            vmem((D, INTO), BF16),
            vmem((D, ALL), BF16),
            vmem((2, 256, RANK), F32),
            vmem((2, 128, RANK), F32),
            vmem((2 * RANK, ALL), BF16),
            vmem((192, TOK), BF16),
            vmem((64, TOK), BF16),
            vmem((TOK, D), F32),
            vmem((2, 4, SHARE, D), F32),
            vmem((D, ALL), BF16),
            vmem((D, ALL), BF16),
            vmem((2, 128, HALF), F32),
            vmem((128, HALF), F32),
            vmem((CHIPS - 1, 8, HALF), F32),
            vmem((2, 128, HALF), F32),
            vmem((2, 32, HALF), F32),
            vmem((256, D), BF16),
            vmem((D, 128), F32),
            vmem((D, 384), BF16),
            vmem((RANK, 1024), F32),
            vmem((N_DP - 1, 8, 128), F32),
            vmem((RANK, 1024), F32),
            vmem((384, ALL), BF16),
            vmem((D, ALL), BF16),
            vmem((SHARE, D), BF16),
            vmem((4, ROWS_P, RANK), F32),
            vmem((2, 256, RANK), F32),
            vmem((2, 128, RANK), F32),
            sems((15,)),
            sems((2, 4, 2)), sems((2, 4, 2)),
            sems((2, 4, 2)), sems((2, 4, 2)),
            sems((2, 4, 2)), sems((2, 4, 2)),
            sems, sems,
            sems((CHIPS - 1,)), sems((CHIPS - 1,)),
            sems((CHIPS - 1,)), sems((CHIPS - 1,)),
            sems, sems,
            sems((N_DP - 1,)), sems((N_DP - 1,)),
            sems((N_DP - 1,)), sems((N_DP - 1,)),
            sems((9, 4)),
            sems((7,)),
        ],
        compiler_params=pltpu.CompilerParams(
            collective_id=0, has_side_effects=True, vmem_limit_bytes=58 * 1024 * 1024
        ),
    )(*args)


def solution(mesh):
    return jax.shard_map(
        on_device,
        mesh=mesh,
        in_specs=(
            P(("dp", "mp"), None),
            P(("dp", "mp"), None),
            P("dp", "mp"),
            P("dp", "mp"),
            P(None, "dp", "mp"),
            P(None, "mp"),
            P(None, None, "mp"),
            P("dp", None, None, "mp"),
            P("dp", None, None, "mp"),
            P(None, "mp", None),
            P(None, "mp", None),
        ),
        out_specs=(
            P(("dp", "mp"), None),
            P(None, "mp", "dp", None),
            P(None, "mp", "dp", None),
            P(None, "mp", None),
            P(None, "mp", None),
            P("dp", None, None, "mp"),
            P("dp", None, None, "mp"),
        ),
        check_vma=False,
    )
```

```python
import jax
import jax.numpy as jnp
from jax import lax
from jax.experimental import pallas as pl
from jax.experimental.pallas import tpu as pltpu
from jax.sharding import PartitionSpec as P

MESH = pl.DeviceIdType.MESH
F32 = jnp.float32
BF16 = jnp.bfloat16

D = 2304
HALF = D // 2
TOK = 512
SHARE = 64
PART = SHARE // 2
FINE = SHARE // 4
RANK = 32
N_DP = 32
N_MP = 8
CHIPS = N_DP // 2
REDUCERS = 12
ROWS_P = D // N_DP
COLS = ((0, 256), (256, 128), (384, 128), (512, 256))
INTO = 512
ALL = 768


def split(value):
    high = value.astype(BF16)
    return high, (value - high.astype(F32)).astype(BF16)


def dot(a, b, on_a=1, on_b=0):
    return lax.dot_general(a, b, (((on_a,), (on_b,)), ((), ())), preferred_element_type=F32)


def kernel(
    x_in, out_grad, context, query_grad, keyval_grad, query_weight, keyval_weight,
    wide_error, narrow_error, wide_start, narrow_start,
    input_grad, wide_p, narrow_p, wide_q, narrow_q, wide_new, narrow_new,
    xf, yf, gv, wv, ev, sw, sn, st, tx, ty, pg, rr, sh, sl,
    fl, ra, rbx, rby, ff, rowbuf, pb, pt, pc, ql, rq, ry, qf, qbd,
    load_sem, x_send, x_recv, y_send, y_recv, z_send, z_recv,
    a_send, a_recv, b_send, b_recv, c_send, c_recv, d_send, d_recv,
    e_send, e_recv, f_send, f_recv, h_send, h_recv,
):
    dp = lax.axis_index("dp")
    mp = lax.axis_index("mp")
    core = dp % 2
    chip = dp // 2
    mate = dp + 1 - 2 * core
    ring = ((mp + 1) % N_MP, (mp + N_MP - 1) % N_MP)

    def along(way, steps):
        return (mp + steps) % N_MP if way == 0 else (mp + N_MP - steps) % N_MP

    loads = [
        (query_grad, gv.at[:, 0:256]),
        (keyval_grad.at[0], gv.at[:, 256:384]),
        (keyval_grad.at[1], gv.at[:, 384:512]),
        (query_weight, wv.at[:, 0:256]),
        (keyval_weight.at[0], wv.at[:, 256:384]),
        (keyval_weight.at[1], wv.at[:, 384:512]),
        (wide_start, sw),
        (narrow_start, sn),
        (wide_error.at[0, 0], ev.at[:, 0:256]),
        (narrow_error.at[0, 0], ev.at[:, 256:384]),
        (narrow_error.at[0, 1], ev.at[:, 384:512]),
        (wide_error.at[0, 1], ev.at[:, 512:768]),
        (context, gv.at[:, 512:768]),
        (x_in, xf.at[pl.ds(pl.multiple_of(mp * SHARE, SHARE), SHARE), :]),
        (out_grad, yf.at[pl.ds(pl.multiple_of(mp * SHARE, SHARE), SHARE), :]),
    ]
    loads = [pltpu.make_async_copy(a, b, load_sem.at[i]) for i, (a, b) in enumerate(loads)]
    for copy in loads:
        copy.start()

    barrier = pltpu.get_barrier_semaphore()
    for way in (0, 1):
        pl.semaphore_signal(barrier, inc=1, device_id=(dp, ring[way]), device_id_type=MESH)

    @pl.loop(1, N_DP)
    def _(k):
        pl.semaphore_signal(barrier, inc=1, device_id=((dp + k) % N_DP, mp), device_id_type=MESH)

    pl.semaphore_wait(barrier, N_DP + 1)

    def hop(own, full, send, recv, way, step, role):
        part = role if way == 0 else 3 - role
        owner = along(1 - way, step - 1)
        rows = pl.ds(pl.multiple_of(owner * SHARE + part * FINE, FINE), FINE)
        src = own.at[part * FINE:(part + 1) * FINE, :] if step == 1 else full.at[rows, :]
        return pltpu.make_async_remote_copy(
            src_ref=src, dst_ref=full.at[rows, :],
            send_sem=send.at[way, step - 1, role], recv_sem=recv.at[way, step - 1, role],
            device_id=(dp, ring[way]), device_id_type=MESH,
        )

    def x_hop(way, step, role):
        return hop(x_in, xf, x_send, x_recv, way, step, role)

    def y_hop(way, step, role):
        return hop(out_grad, yf, y_send, y_recv, way, step, role)

    def first(make, roles=(0, 1, 2, 3)):
        for role in roles:
            for way in (0, 1):
                make(way, 1, role).start()

    def forward(make, step, *roles):
        for role in roles:
            for way in (0, 1):
                make(way, step - 1, role).wait_recv()
                make(way, step, role).start()

    def finish_ring(make):
        for step, role in ((3, 2), (3, 3), (4, 0), (4, 1)):
            for way in (0, 1):
                make(way, step, role).wait_recv()

    def drain_ring(make):
        for way in (0, 1):
            for step in (1, 2, 3, 4):
                for role in (0, 1, 2, 3):
                    if step < 4 or role < 2:
                        make(way, step, role).wait_send()

    def z_hop(way, step, role):
        part = way if role == 0 else 1 - way
        dest = along(way, 5 - step)
        rows = pl.ds(pl.multiple_of(dest * SHARE + part * PART, PART), PART)
        here = slice(part * PART, (part + 1) * PART)
        if step == (1 if role == 0 else 2):
            src = pg.at[rows, :]
        else:
            src = rr.at[way, step - 2, here, :]
        return pltpu.make_async_remote_copy(
            src_ref=src, dst_ref=rr.at[way, step - 1, here, :],
            send_sem=z_send.at[way, step - 1, role], recv_sem=z_recv.at[way, step - 1, role],
            device_id=(dp, ring[way]), device_id_type=MESH,
        ), rows, here

    def z_first():
        for way in (0, 1):
            z_hop(way, 1, 0)[0].start()
        for way in (0, 1):
            z_hop(way, 2, 1)[0].start()

    def z_step(step, role):
        for way in (0, 1):
            z_hop(way, step - 1, role)[0].wait_recv()
            copy, rows, here = z_hop(way, step, role)
            rr[way, step - 2, here, :] += pg[rows, :]
            copy.start()

    x_rows = slice(0, 96)
    y_rows = slice(96, 128)

    def chunk(group, p):
        if group == 0:
            return pl.ds(pl.multiple_of(p * 8, 8), 8), pl.ds(0, HALF)
        return (
            pl.ds(pl.multiple_of(96 + (p // 3) * 8, 8), 8),
            pl.ds(pl.multiple_of((p % 3) * 384, 384), 384),
        )

    def a_copy(group):
        rows = (x_rows, y_rows)[group]
        return pltpu.make_async_remote_copy(
            src_ref=fl.at[1 - core, rows], dst_ref=ra.at[rows],
            send_sem=a_send.at[group], recv_sem=a_recv.at[group],
            device_id=(mate, mp), device_id_type=MESH,
        )

    def b_copy(group, k, other):
        rows, lanes = chunk(group, other)
        return pltpu.make_async_remote_copy(
            src_ref=fl.at[core, rows, lanes], dst_ref=(rbx, rby)[group].at[k - 1],
            send_sem=b_send.at[group, k - 1], recv_sem=b_recv.at[group, k - 1],
            device_id=(2 * other + core, mp), device_id_type=MESH,
        )

    def c_copy(group, k, other, source):
        rows, lanes = chunk(group, source)
        own = ff.at[core, rows, lanes]
        return pltpu.make_async_remote_copy(
            src_ref=own, dst_ref=own,
            send_sem=c_send.at[group, k - 1], recv_sem=c_recv.at[group, k - 1],
            device_id=(2 * other + core, mp), device_id_type=MESH,
        )

    def d_copy(group):
        own = ff.at[core, (x_rows, y_rows)[group]]
        return pltpu.make_async_remote_copy(
            src_ref=own, dst_ref=own, send_sem=d_send.at[group], recv_sem=d_recv.at[group],
            device_id=(mate, mp), device_id_type=MESH,
        )

    def to_reducers(group):
        rows = (x_rows, y_rows)[group]
        a_copy(group).wait_recv()
        fl[core, rows] += ra[rows]

        @pl.loop(1, CHIPS)
        def _(k):
            other = (chip + k) % CHIPS

            @pl.when(other < REDUCERS)
            def _():
                b_copy(group, k, other).start()

    def from_reducers(group):
        @pl.when(chip < REDUCERS)
        def _():
            @pl.loop(1, CHIPS)
            def _(k):
                b_copy(group, k, chip).wait_recv()

            rows, lanes = chunk(group, chip)
            ff[core, rows, lanes] = fl[core, rows, lanes] + jnp.sum((rbx, rby)[group][...], axis=0)

            @pl.loop(1, CHIPS)
            def _(k):
                c_copy(group, k, (chip + k) % CHIPS, chip).start()

    def to_mate(group):
        @pl.loop(1, CHIPS)
        def _(k):
            source = (chip + CHIPS - k) % CHIPS

            @pl.when(source < REDUCERS)
            def _():
                c_copy(group, k, chip, source).wait_recv()

        d_copy(group).start()

    def from_mate(group):
        a_copy(group).wait_send()

        @pl.loop(1, CHIPS)
        def _(k):
            other = (chip + k) % CHIPS

            @pl.when(other < REDUCERS)
            def _():
                b_copy(group, k, other).wait_send()

        @pl.when(chip < REDUCERS)
        def _():
            @pl.loop(1, CHIPS)
            def _(k):
                c_copy(group, k, (chip + k) % CHIPS, chip).wait_send()

        d_copy(group).wait()

    first(x_hop)
    for i in range(6):
        loads[i].wait()

    def partial_input_grad(start, stop):
        @pl.loop(start, stop)
        def _(j):
            cols = pl.ds(pl.multiple_of(j * 256, 256), 256)
            pg[:, cols] = dot(gv[:, 0:INTO], wv[cols, :], 1, 1)

    partial_input_grad(0, 3)
    forward(x_hop, 2, 0, 1)
    partial_input_grad(3, 6)
    forward(x_hop, 2, 2, 3)
    partial_input_grad(6, 9)
    forward(x_hop, 3, 0)

    for i in (6, 7):
        loads[i].wait()
    for b, (at, width) in enumerate(COLS):
        high, low = split(sw[0 if b == 0 else 1] if width == 256 else sn[b - 1])
        st[0:RANK, at:at + width] = high
        st[RANK:2 * RANK, at:at + width] = low
    loads[12].wait()
    for b, (at, width) in enumerate(COLS):
        t = dot(st[:, at:at + width], gv[:, at:at + width], 1, 1)
        high, low = split(t[:RANK] + t[RANK:])
        if b < 3:
            tx[b * RANK:(b + 1) * RANK, :] = high
            tx[96 + b * RANK:96 + (b + 1) * RANK, :] = low
        else:
            ty[0:RANK, :] = high
            ty[RANK:2 * RANK, :] = low
    qbd[...] = jnp.zeros_like(qbd)

    forward(x_hop, 3, 1)
    for i in (8, 9, 10, 11):
        loads[i].wait()

    def error_factors(start, stop):
        @pl.loop(start, stop)
        def _(j):
            rows = pl.ds(pl.multiple_of(j * 384, 384), 384)
            lanes = pl.ds(pl.multiple_of((j % 3) * 384, 384), 384)
            for b, (at, width) in enumerate(COLS):
                e = dot(st[:, at:at + width], ev[rows, at:at + width], 1, 1)
                fl[j // 3, b * RANK:(b + 1) * RANK, lanes] = e[:RANK] + e[RANK:]

    error_factors(0, 3)
    forward(x_hop, 3, 2)
    error_factors(3, 6)
    forward(x_hop, 3, 3)
    forward(x_hop, 4, 0, 1)
    first(y_hop)
    loads[13].wait()
    finish_ring(x_hop)

    @pl.loop(0, 6)
    def _(j):
        cols = pl.ds(pl.multiple_of(j * 384, 384), 384)
        lanes = pl.ds(pl.multiple_of((j % 3) * 384, 384), 384)
        f = dot(tx[...], xf[:, cols])
        fl[j // 3, 0:96, lanes] += f[:96] + f[96:]

    a_copy(0).start()

    def sums_into(start, stop):
        @pl.loop(start, stop)
        def _(j):
            rows = pl.ds(pl.multiple_of(j * 256, 256), 256)
            total = dot(xf[:, rows], gv[:, 0:INTO], 0, 0) + ev[rows, 0:INTO].astype(F32)
            high, low = split(total)
            sh[rows, 0:INTO] = high
            sl[rows, 0:INTO] = low

    forward(y_hop, 2, 0, 1)
    to_reducers(0)
    forward(y_hop, 2, 2, 3)
    sums_into(0, 3)
    forward(y_hop, 3, 0, 1)
    from_reducers(0)
    sums_into(3, 6)
    forward(y_hop, 3, 2)
    sums_into(6, 9)
    forward(y_hop, 3, 3)
    to_mate(0)
    forward(y_hop, 4, 0, 1)
    z_first()
    loads[14].wait()
    from_mate(0)
    finish_ring(y_hop)

    @pl.loop(0, 6)
    def _(j):
        cols = pl.ds(pl.multiple_of(j * 384, 384), 384)
        lanes = pl.ds(pl.multiple_of((j % 3) * 384, 384), 384)
        f = dot(ty[...], yf[:, cols])
        fl[j // 3, 96:128, lanes] += f[:RANK] + f[RANK:]

    a_copy(1).start()

    def gram_schmidt(block, which):
        @pl.loop(0, 8)
        def _(i):
            norms = {}
            for b in which:
                row = [ff[h, pl.ds(b * RANK + block * 8 + i, 1), :] for h in (0, 1)]
                for h in (0, 1):
                    rowbuf[h, b * 8:b * 8 + 8, :] = jnp.broadcast_to(row[h], (8, HALF))
                norms[b] = jnp.sum(row[0] * row[0] + row[1] * row[1], axis=1, keepdims=True)
            later = lax.broadcasted_iota(jnp.int32, (8, 1), 0) > i
            scales = {}
            for b in which:
                for t in range(block, 4):
                    at = slice(b * RANK + t * 8, b * RANK + t * 8 + 8)
                    r = slice(b * 8, b * 8 + 8)
                    dots = jnp.sum(
                        ff[0, at, :] * rowbuf[0, r, :] + ff[1, at, :] * rowbuf[1, r, :],
                        axis=1, keepdims=True,
                    )
                    scale = dots / norms[b]
                    scales[b, t] = jnp.where(later, scale, 0.0) if t == block else scale
            for b in which:
                for t in range(block, 4):
                    at = slice(b * RANK + t * 8, b * RANK + t * 8 + 8)
                    for h in (0, 1):
                        ff[h, at, :] -= scales[b, t] * rowbuf[h, b * 8:b * 8 + 8, :]

    def right_factors(which):
        for b in which:
            at = slice(b * RANK, (b + 1) * RANK)
            squares = jnp.sum(
                ff[0, at, :] * ff[0, at, :] + ff[1, at, :] * ff[1, at, :], axis=1, keepdims=True
            )
            size = jnp.sqrt(squares)
            for h in (0, 1):
                unit = ff[h, at, :] / size
                ff[h, at, :] = unit
                high, low = split(unit)
                pb[2 * b * RANK:(2 * b + 1) * RANK, h * HALF:(h + 1) * HALF] = high
                pb[(2 * b + 1) * RANK:(2 * b + 2) * RANK, h * HALF:(h + 1) * HALF] = low
        for b in which:
            at, width = COLS[b]
            both = dot(pb[2 * b * RANK:(2 * b + 2) * RANK, :], sh[:, at:at + width])
            rest = dot(pb[2 * b * RANK:(2 * b + 1) * RANK, :], sl[:, at:at + width])
            ql[:, at:at + width] = both[:RANK] + both[RANK:] + rest

    into = (0, 1, 2)
    outof = (3,)

    @pl.loop(0, 9)
    def _(j):
        rows = pl.ds(pl.multiple_of(j * 256, 256), 256)
        total = dot(yf[:, rows], gv[:, INTO:ALL], 0, 0) + ev[rows, INTO:ALL].astype(F32)
        high, low = split(total)
        sh[rows, INTO:ALL] = high
        sl[rows, INTO:ALL] = low

    to_reducers(1)
    z_step(2, 0)
    gram_schmidt(0, into)
    from_reducers(1)
    gram_schmidt(1, into)
    z_step(3, 1)
    gram_schmidt(2, into)
    gram_schmidt(3, into)
    to_mate(1)
    right_factors(into)
    from_mate(1)
    z_step(3, 0)
    gram_schmidt(0, outof)
    gram_schmidt(1, outof)
    gram_schmidt(2, outof)
    gram_schmidt(3, outof)
    right_factors(outof)

    place = dp % 8
    line = dp // 8

    def part_of(j):
        return (
            pl.ds(pl.multiple_of((j % 4) * 8, 8), 8),
            pl.ds(pl.multiple_of((j // 4) * 384, 384), 384),
        )

    own_part = part_of(place)

    def e_copy(k):
        other = (place + k) % 8
        rows, lanes = part_of(other)
        return pltpu.make_async_remote_copy(
            src_ref=ql.at[rows, lanes], dst_ref=rq.at[k - 1],
            send_sem=e_send.at[k - 1], recv_sem=e_recv.at[k - 1],
            device_id=(line * 8 + other, mp), device_id_type=MESH,
        )

    def f_copy(k):
        return pltpu.make_async_remote_copy(
            src_ref=ry.at[line], dst_ref=ry.at[line],
            send_sem=f_send.at[k - 1], recv_sem=f_recv.at[k - 1],
            device_id=(((line + k) % 4) * 8 + place, mp), device_id_type=MESH,
        )

    def h_copy(k):
        own = qf.at[own_part[0], own_part[1]]
        return pltpu.make_async_remote_copy(
            src_ref=own, dst_ref=own,
            send_sem=h_send.at[k - 1], recv_sem=h_recv.at[k - 1],
            device_id=(line * 8 + (place + k) % 8, mp), device_id_type=MESH,
        )

    @pl.loop(1, 8)
    def _(k):
        e_copy(k).start()

    for h in (0, 1):
        @pl.loop(0, 3)
        def _(j):
            lanes = pl.ds(pl.multiple_of(j * 384, 384), 384)
            rows = pl.ds(pl.multiple_of(h * HALF + j * 384, 384), 384)
            by_row = jnp.transpose(ff[h, :, lanes])
            pt[rows, :] = by_row
            high, low = split(by_row)
            pc[rows, 0:128] = high
            pc[rows, 128:256] = high
            pc[rows, 256:384] = low

    @pl.loop(1, 8)
    def _(k):
        e_copy(k).wait_recv()

    ry[line] = ql[own_part[0], own_part[1]] + jnp.sum(rq[...], axis=0)

    @pl.loop(1, 4)
    def _(k):
        f_copy(k).start()

    z_step(4, 1)

    @pl.loop(1, 4)
    def _(k):
        f_copy(k).wait_recv()

    qf[own_part[0], own_part[1]] = (ry[0] + ry[1] + ry[2] + ry[3]) * (1.0 / N_DP)

    @pl.loop(1, 8)
    def _(k):
        h_copy(k).start()

    mine = jnp.transpose(pt[pl.ds(pl.multiple_of(dp * ROWS_P, 8), ROWS_P), :])
    for b, ref in enumerate((wide_p.at[0], narrow_p.at[0], narrow_p.at[1], wide_p.at[1])):
        ref[0] = mine[b * RANK:(b + 1) * RANK]

    @pl.loop(1, 8)
    def _(k):
        h_copy(k).wait_recv()

    for b, (at, width) in enumerate(COLS):
        q = qf[:, at:at + width]
        (wide_q, narrow_q)[width == 128][(0, 0, 1, 1)[b]] = q
        high, low = split(q)
        qbd[b * RANK:(b + 1) * RANK, at:at + width] = high
        qbd[128 + b * RANK:128 + (b + 1) * RANK, at:at + width] = low
        qbd[256 + b * RANK:256 + (b + 1) * RANK, at:at + width] = high

    z_step(4, 0)

    @pl.loop(0, 9)
    def _(j):
        rows = pl.ds(pl.multiple_of(j * 256, 256), 256)
        low_rank = dot(pc[rows, :], qbd[...])
        new = (sh[rows, :].astype(F32) + sl[rows, :].astype(F32) - low_rank).astype(BF16)
        for b, ref in enumerate((wide_new, narrow_new, narrow_new, wide_new)):
            at, width = COLS[b]
            ref[0, (0, 0, 1, 1)[b], rows, :] = new[:, at:at + width]

    for way in (0, 1):
        for role in (0, 1):
            z_hop(way, 4, role)[0].wait_recv()
    own = pl.ds(pl.multiple_of(mp * SHARE, SHARE), SHARE)
    input_grad[...] = (pg[own, :] + rr[0, 3] + rr[1, 3]).astype(BF16)

    drain_ring(x_hop)
    drain_ring(y_hop)
    for way in (0, 1):
        for step in (1, 2, 3, 4):
            for role in (0, 1):
                if (step, role) != (1, 1):
                    z_hop(way, step, role)[0].wait_send()

    @pl.loop(1, 8)
    def _(k):
        e_copy(k).wait_send()
        h_copy(k).wait_send()

    @pl.loop(1, 4)
    def _(k):
        f_copy(k).wait_send()


def hand_out(*refs):
    sources, targets, sem = refs[:7], refs[7:14], refs[14]
    copies = [pltpu.make_async_copy(a, b, sem.at[i]) for i, (a, b) in enumerate(zip(sources, targets))]
    for copy in copies:
        copy.start()
    for copy in copies:
        copy.wait()


def on_device(*args):
    sems = pltpu.SemaphoreType.DMA
    vmem = pltpu.VMEM
    args = args[:9] + tuple(jnp.swapaxes(a, 1, 2) for a in args[9:])
    shapes = (
        ((SHARE, D), BF16),
        ((2, 1, RANK, ROWS_P), F32),
        ((2, 1, RANK, ROWS_P), F32),
        ((2, RANK, 256), F32),
        ((2, RANK, 128), F32),
        ((1, 2, D, 256), BF16),
        ((1, 2, D, 128), BF16),
    )
    outs = pl.pallas_call(
        kernel,
        out_shape=tuple(pltpu.VMEM(shape, dtype) for shape, dtype in shapes),
        in_specs=[pl.BlockSpec(memory_space=pltpu.HBM)] * 11,
        out_specs=tuple([pl.BlockSpec(memory_space=pltpu.VMEM)] * 7),
        scratch_shapes=[
            vmem((TOK, D), BF16),
            vmem((TOK, D), BF16),
            vmem((TOK, ALL), BF16),
            vmem((D, INTO), BF16),
            vmem((D, ALL), BF16),
            vmem((2, RANK, 256), F32),
            vmem((2, RANK, 128), F32),
            vmem((2 * RANK, ALL), BF16),
            vmem((192, TOK), BF16),
            vmem((64, TOK), BF16),
            vmem((TOK, D), F32),
            vmem((2, 4, SHARE, D), F32),
            vmem((D, ALL), BF16),
            vmem((D, ALL), BF16),
            vmem((2, 128, HALF), F32),
            vmem((128, HALF), F32),
            vmem((CHIPS - 1, 8, HALF), F32),
            vmem((CHIPS - 1, 8, 384), F32),
            vmem((2, 128, HALF), F32),
            vmem((2, 32, HALF), F32),
            vmem((256, D), BF16),
            vmem((D, 128), F32),
            vmem((D, 384), BF16),
            vmem((RANK, ALL), F32),
            vmem((7, 8, 384), F32),
            vmem((4, 8, 384), F32),
            vmem((RANK, ALL), F32),
            vmem((384, ALL), BF16),
            sems((15,)),
            sems((2, 4, 4)), sems((2, 4, 4)),
            sems((2, 4, 4)), sems((2, 4, 4)),
            sems((2, 4, 2)), sems((2, 4, 2)),
            sems((2,)), sems((2,)),
            sems((2, CHIPS - 1)), sems((2, CHIPS - 1)),
            sems((2, CHIPS - 1)), sems((2, CHIPS - 1)),
            sems((2,)), sems((2,)),
            sems((7,)), sems((7,)),
            sems((3,)), sems((3,)),
            sems((7,)), sems((7,)),
        ],
        compiler_params=pltpu.CompilerParams(
            collective_id=0, has_side_effects=True, vmem_limit_bytes=59 * 1024 * 1024
        ),
    )(*args)
    outs = pl.pallas_call(
        hand_out,
        out_shape=tuple(jax.ShapeDtypeStruct(shape, dtype) for shape, dtype in shapes),
        in_specs=[pl.BlockSpec(memory_space=pltpu.VMEM)] * 7,
        out_specs=tuple([pl.BlockSpec(memory_space=pl.ANY)] * 7),
        scratch_shapes=[sems((7,))],
        compiler_params=pltpu.CompilerParams(vmem_limit_bytes=16 * 1024 * 1024),
    )(*outs)
    turned = [jnp.swapaxes(a, -1, -2) for a in outs[1:5]]
    return (outs[0], *turned, *outs[5:])


def solution(mesh):
    return jax.shard_map(
        on_device,
        mesh=mesh,
        in_specs=(
            P(("dp", "mp"), None),
            P(("dp", "mp"), None),
            P("dp", "mp"),
            P("dp", "mp"),
            P(None, "dp", "mp"),
            P(None, "mp"),
            P(None, None, "mp"),
            P("dp", None, None, "mp"),
            P("dp", None, None, "mp"),
            P(None, "mp", None),
            P(None, "mp", None),
        ),
        out_specs=(
            P(("dp", "mp"), None),
            P(None, "mp", "dp", None),
            P(None, "mp", "dp", None),
            P(None, "mp", None),
            P(None, "mp", None),
            P("dp", None, None, "mp"),
            P("dp", None, None, "mp"),
        ),
        check_vma=False,
    )
```

```python
import jax
import jax.numpy as jnp
from jax import lax
from jax.experimental import pallas as pl
from jax.experimental.pallas import tpu as pltpu
from jax.sharding import PartitionSpec as P

MESH = pl.DeviceIdType.MESH
F32 = jnp.float32
BF16 = jnp.bfloat16

D = 2304
HALF = D // 2
TOK = 512
SHARE = 64
PART = SHARE // 2
FINE = SHARE // 4
RANK = 32
N_DP = 32
N_MP = 8
CHIPS = N_DP // 2
REDUCERS = 12
ROWS_P = D // N_DP
COLS = ((0, 256), (256, 128), (384, 128), (512, 256))
INTO = 512
ALL = 768


def split(value):
    high = value.astype(BF16)
    return high, (value - high.astype(F32)).astype(BF16)


def dot(a, b, on_a=1, on_b=0):
    return lax.dot_general(a, b, (((on_a,), (on_b,)), ((), ())), preferred_element_type=F32)


def kernel(
    x_in, out_grad, context, query_grad, keyval_grad, query_weight, keyval_weight,
    wide_error, narrow_error, wide_start, narrow_start,
    input_grad, wide_p, narrow_p, wide_q, narrow_q, wide_new, narrow_new,
    xf, yf, gv, wv, ev, sw, sn, st, tx, ty, pg, rr, sh, sl,
    fl, ra, rbx, rby, ff, rowbuf, pb, pt, pc, ql, rq, ry, qf, qbd,
    load_sem, x_send, x_recv, y_send, y_recv, z_send, z_recv,
    a_send, a_recv, b_send, b_recv, c_send, c_recv, d_send, d_recv,
    e_send, e_recv, f_send, f_recv, h_send, h_recv,
):
    dp = lax.axis_index("dp")
    mp = lax.axis_index("mp")
    core = dp % 2
    chip = dp // 2
    mate = dp + 1 - 2 * core
    ring = ((mp + 1) % N_MP, (mp + N_MP - 1) % N_MP)

    def along(way, steps):
        return (mp + steps) % N_MP if way == 0 else (mp + N_MP - steps) % N_MP

    loads = [
        (query_grad, gv.at[:, 0:256]),
        (keyval_grad.at[0], gv.at[:, 256:384]),
        (keyval_grad.at[1], gv.at[:, 384:512]),
        (query_weight, wv.at[:, 0:256]),
        (keyval_weight.at[0], wv.at[:, 256:384]),
        (keyval_weight.at[1], wv.at[:, 384:512]),
        (wide_start, sw),
        (narrow_start, sn),
        (wide_error.at[0, 0], ev.at[:, 0:256]),
        (narrow_error.at[0, 0], ev.at[:, 256:384]),
        (narrow_error.at[0, 1], ev.at[:, 384:512]),
        (wide_error.at[0, 1], ev.at[:, 512:768]),
        (context, gv.at[:, 512:768]),
        (x_in, xf.at[pl.ds(pl.multiple_of(mp * SHARE, SHARE), SHARE), :]),
        (out_grad, yf.at[pl.ds(pl.multiple_of(mp * SHARE, SHARE), SHARE), :]),
    ]
    loads = [pltpu.make_async_copy(a, b, load_sem.at[i]) for i, (a, b) in enumerate(loads)]
    for i in range(6):
        loads[i].start()

    barrier = pltpu.get_barrier_semaphore()
    for way in (0, 1):
        pl.semaphore_signal(barrier, inc=1, device_id=(dp, ring[way]), device_id_type=MESH)

    @pl.loop(1, CHIPS)
    def _(k):
        other = 2 * ((chip + k) % CHIPS) + core
        pl.semaphore_signal(barrier, inc=1, device_id=(other, mp), device_id_type=MESH)

    @pl.loop(0, 4)
    def _(k):
        other = (dp // 8) * 8 + 2 * k + 1 - core
        pl.semaphore_signal(barrier, inc=1, device_id=(other, mp), device_id_type=MESH)

    pl.semaphore_wait(barrier, 2 + (CHIPS - 1) + 4)

    def hop(own, full, send, recv, way, step, role):
        part = role if way == 0 else 3 - role
        owner = along(1 - way, step - 1)
        rows = pl.ds(pl.multiple_of(owner * SHARE + part * FINE, FINE), FINE)
        src = own.at[part * FINE:(part + 1) * FINE, :] if step == 1 else full.at[rows, :]
        return pltpu.make_async_remote_copy(
            src_ref=src, dst_ref=full.at[rows, :],
            send_sem=send.at[way, step - 1, role], recv_sem=recv.at[way, step - 1, role],
            device_id=(dp, ring[way]), device_id_type=MESH,
        )

    def x_hop(way, step, role):
        return hop(x_in, xf, x_send, x_recv, way, step, role)

    def y_hop(way, step, role):
        return hop(out_grad, yf, y_send, y_recv, way, step, role)

    def first(make, roles=(0, 1, 2, 3)):
        for role in roles:
            for way in (0, 1):
                make(way, 1, role).start()

    def forward(make, step, *roles):
        for role in roles:
            for way in (0, 1):
                make(way, step - 1, role).wait_recv()
                make(way, step, role).start()

    def finish_ring(make):
        for step, role in ((3, 2), (3, 3), (4, 0), (4, 1)):
            for way in (0, 1):
                make(way, step, role).wait_recv()

    def drain_ring(make):
        for way in (0, 1):
            for step in (1, 2, 3, 4):
                for role in (0, 1, 2, 3):
                    if step < 4 or role < 2:
                        make(way, step, role).wait_send()

    def z_hop(way, step, role):
        part = way if role == 0 else 1 - way
        dest = along(way, 5 - step)
        rows = pl.ds(pl.multiple_of(dest * SHARE + part * PART, PART), PART)
        here = slice(part * PART, (part + 1) * PART)
        if step == (1 if role == 0 else 2):
            src = pg.at[rows, :]
        else:
            src = rr.at[way, step - 2, here, :]
        return pltpu.make_async_remote_copy(
            src_ref=src, dst_ref=rr.at[way, step - 1, here, :],
            send_sem=z_send.at[way, step - 1, role], recv_sem=z_recv.at[way, step - 1, role],
            device_id=(dp, ring[way]), device_id_type=MESH,
        ), rows, here

    def z_first(step, role):
        for way in (0, 1):
            z_hop(way, step, role)[0].start()

    def z_step(step, role):
        for way in (0, 1):
            z_hop(way, step - 1, role)[0].wait_recv()
            copy, rows, here = z_hop(way, step, role)
            rr[way, step - 2, here, :] += pg[rows, :]
            copy.start()

    x_rows = slice(0, 96)
    y_rows = slice(96, 128)

    def chunk(group, p):
        if group == 0:
            return pl.ds(pl.multiple_of(p * 8, 8), 8), pl.ds(0, HALF)
        return (
            pl.ds(pl.multiple_of(96 + (p // 3) * 8, 8), 8),
            pl.ds(pl.multiple_of((p % 3) * 384, 384), 384),
        )

    def a_copy(group):
        rows = (x_rows, y_rows)[group]
        return pltpu.make_async_remote_copy(
            src_ref=fl.at[1 - core, rows], dst_ref=ra.at[rows],
            send_sem=a_send.at[group], recv_sem=a_recv.at[group],
            device_id=(mate, mp), device_id_type=MESH,
        )

    def b_copy(group, k, other):
        rows, lanes = chunk(group, other)
        return pltpu.make_async_remote_copy(
            src_ref=fl.at[core, rows, lanes], dst_ref=(rbx, rby)[group].at[k - 1],
            send_sem=b_send.at[group, k - 1], recv_sem=b_recv.at[group, k - 1],
            device_id=(2 * other + core, mp), device_id_type=MESH,
        )

    def c_copy(group, k, other, source):
        rows, lanes = chunk(group, source)
        own = ff.at[core, rows, lanes]
        return pltpu.make_async_remote_copy(
            src_ref=own, dst_ref=own,
            send_sem=c_send.at[group, k - 1], recv_sem=c_recv.at[group, k - 1],
            device_id=(2 * other + core, mp), device_id_type=MESH,
        )

    def d_copy(group):
        own = ff.at[core, (x_rows, y_rows)[group]]
        return pltpu.make_async_remote_copy(
            src_ref=own, dst_ref=own, send_sem=d_send.at[group], recv_sem=d_recv.at[group],
            device_id=(mate, mp), device_id_type=MESH,
        )

    def to_reducers(group):
        rows = (x_rows, y_rows)[group]
        a_copy(group).wait_recv()
        fl[core, rows] += ra[rows]

        @pl.loop(1, CHIPS)
        def _(k):
            other = (chip + k) % CHIPS

            @pl.when(other < REDUCERS)
            def _():
                b_copy(group, k, other).start()

    def from_reducers(group):
        @pl.when(chip < REDUCERS)
        def _():
            @pl.loop(1, CHIPS)
            def _(k):
                b_copy(group, k, chip).wait_recv()

            rows, lanes = chunk(group, chip)
            ff[core, rows, lanes] = fl[core, rows, lanes] + jnp.sum((rbx, rby)[group][...], axis=0)

            @pl.loop(1, CHIPS)
            def _(k):
                c_copy(group, k, (chip + k) % CHIPS, chip).start()

    def to_mate(group):
        @pl.loop(1, CHIPS)
        def _(k):
            source = (chip + CHIPS - k) % CHIPS

            @pl.when(source < REDUCERS)
            def _():
                c_copy(group, k, chip, source).wait_recv()

        d_copy(group).start()

    def from_mate(group):
        a_copy(group).wait_send()

        @pl.loop(1, CHIPS)
        def _(k):
            other = (chip + k) % CHIPS

            @pl.when(other < REDUCERS)
            def _():
                b_copy(group, k, other).wait_send()

        @pl.when(chip < REDUCERS)
        def _():
            @pl.loop(1, CHIPS)
            def _(k):
                c_copy(group, k, (chip + k) % CHIPS, chip).wait_send()

        d_copy(group).wait()

    first(x_hop)
    for copy in loads[6:]:
        copy.start()
    for i in range(6):
        loads[i].wait()

    def partial_input_grad(start, stop):
        @pl.loop(start, stop)
        def _(j):
            cols = pl.ds(pl.multiple_of(j * 256, 256), 256)
            pg[:, cols] = dot(gv[:, 0:INTO], wv[cols, :], 1, 1)

    partial_input_grad(0, 3)
    forward(x_hop, 2, 0, 1)
    partial_input_grad(3, 6)
    forward(x_hop, 2, 2, 3)
    partial_input_grad(6, 9)
    forward(x_hop, 3, 0)

    for i in (6, 7):
        loads[i].wait()
    for b, (at, width) in enumerate(COLS):
        high, low = split(sw[0 if b == 0 else 1] if width == 256 else sn[b - 1])
        st[0:RANK, at:at + width] = high
        st[RANK:2 * RANK, at:at + width] = low
    loads[12].wait()
    for b, (at, width) in enumerate(COLS):
        t = dot(st[:, at:at + width], gv[:, at:at + width], 1, 1)
        high, low = split(t[:RANK] + t[RANK:])
        if b < 3:
            tx[b * RANK:(b + 1) * RANK, :] = high
            tx[96 + b * RANK:96 + (b + 1) * RANK, :] = low
        else:
            ty[0:RANK, :] = high
            ty[RANK:2 * RANK, :] = low
    qbd[...] = jnp.zeros_like(qbd)

    forward(x_hop, 3, 1)
    for i in (8, 9, 10, 11):
        loads[i].wait()

    def error_factors(start, stop):
        @pl.loop(start, stop)
        def _(j):
            rows = pl.ds(pl.multiple_of(j * 384, 384), 384)
            lanes = pl.ds(pl.multiple_of((j % 3) * 384, 384), 384)
            for b, (at, width) in enumerate(COLS):
                e = dot(st[:, at:at + width], ev[rows, at:at + width], 1, 1)
                fl[j // 3, b * RANK:(b + 1) * RANK, lanes] = e[:RANK] + e[RANK:]

    error_factors(0, 3)
    forward(x_hop, 3, 2)
    error_factors(3, 6)
    forward(x_hop, 3, 3)
    forward(x_hop, 4, 0, 1)
    first(y_hop)
    loads[13].wait()
    finish_ring(x_hop)

    @pl.loop(0, 6)
    def _(j):
        cols = pl.ds(pl.multiple_of(j * 384, 384), 384)
        lanes = pl.ds(pl.multiple_of((j % 3) * 384, 384), 384)
        f = dot(tx[...], xf[:, cols])
        fl[j // 3, 0:96, lanes] += f[:96] + f[96:]

    a_copy(0).start()

    def sums_into(start, stop):
        @pl.loop(start, stop)
        def _(j):
            rows = pl.ds(pl.multiple_of(j * 256, 256), 256)
            total = dot(xf[:, rows], gv[:, 0:INTO], 0, 0) + ev[rows, 0:INTO].astype(F32)
            high, low = split(total)
            sh[rows, 0:INTO] = high
            sl[rows, 0:INTO] = low

    forward(y_hop, 2, 0, 1, 2)
    forward(y_hop, 2, 3)
    sums_into(0, 3)
    to_reducers(0)
    forward(y_hop, 3, 0)
    sums_into(3, 6)
    forward(y_hop, 3, 1)
    sums_into(6, 9)
    forward(y_hop, 3, 2, 3)
    forward(y_hop, 4, 0, 1)
    from_reducers(0)
    loads[14].wait()
    finish_ring(y_hop)
    z_first(1, 0)

    @pl.loop(0, 6)
    def _(j):
        cols = pl.ds(pl.multiple_of(j * 384, 384), 384)
        lanes = pl.ds(pl.multiple_of((j % 3) * 384, 384), 384)
        f = dot(ty[...], yf[:, cols])
        fl[j // 3, 96:128, lanes] += f[:RANK] + f[RANK:]

    a_copy(1).start()
    z_first(2, 1)
    to_mate(0)

    def gram_schmidt(block, which):
        @pl.loop(0, 8)
        def _(i):
            norms = {}
            for b in which:
                row = [ff[h, pl.ds(b * RANK + block * 8 + i, 1), :] for h in (0, 1)]
                for h in (0, 1):
                    rowbuf[h, b * 8:b * 8 + 8, :] = jnp.broadcast_to(row[h], (8, HALF))
                norms[b] = jnp.sum(row[0] * row[0] + row[1] * row[1], axis=1, keepdims=True)
            later = lax.broadcasted_iota(jnp.int32, (8, 1), 0) > i
            scales = {}
            for b in which:
                for t in range(block, 4):
                    at = slice(b * RANK + t * 8, b * RANK + t * 8 + 8)
                    r = slice(b * 8, b * 8 + 8)
                    dots = jnp.sum(
                        ff[0, at, :] * rowbuf[0, r, :] + ff[1, at, :] * rowbuf[1, r, :],
                        axis=1, keepdims=True,
                    )
                    scale = dots / norms[b]
                    scales[b, t] = jnp.where(later, scale, 0.0) if t == block else scale
            for b in which:
                for t in range(block, 4):
                    at = slice(b * RANK + t * 8, b * RANK + t * 8 + 8)
                    for h in (0, 1):
                        ff[h, at, :] -= scales[b, t] * rowbuf[h, b * 8:b * 8 + 8, :]

    def right_factors(which):
        for b in which:
            at = slice(b * RANK, (b + 1) * RANK)
            squares = jnp.sum(
                ff[0, at, :] * ff[0, at, :] + ff[1, at, :] * ff[1, at, :], axis=1, keepdims=True
            )
            size = jnp.sqrt(squares)
            for h in (0, 1):
                unit = ff[h, at, :] / size
                ff[h, at, :] = unit
                high, low = split(unit)
                pb[2 * b * RANK:(2 * b + 1) * RANK, h * HALF:(h + 1) * HALF] = high
                pb[(2 * b + 1) * RANK:(2 * b + 2) * RANK, h * HALF:(h + 1) * HALF] = low
        for b in which:
            at, width = COLS[b]
            both = dot(pb[2 * b * RANK:(2 * b + 2) * RANK, :], sh[:, at:at + width])
            rest = dot(pb[2 * b * RANK:(2 * b + 1) * RANK, :], sl[:, at:at + width])
            ql[:, at:at + width] = both[:RANK] + both[RANK:] + rest

    into = (0, 1, 2)
    outof = (3,)

    @pl.loop(0, 9)
    def _(j):
        rows = pl.ds(pl.multiple_of(j * 256, 256), 256)
        total = dot(yf[:, rows], gv[:, INTO:ALL], 0, 0) + ev[rows, INTO:ALL].astype(F32)
        high, low = split(total)
        sh[rows, INTO:ALL] = high
        sl[rows, INTO:ALL] = low

    to_reducers(1)
    from_mate(0)
    gram_schmidt(0, into)
    from_reducers(1)
    gram_schmidt(1, into)
    gram_schmidt(2, into)
    z_step(2, 0)
    gram_schmidt(3, into)
    to_mate(1)
    right_factors(into)
    from_mate(1)
    z_step(3, 1)
    gram_schmidt(0, outof)
    gram_schmidt(1, outof)
    gram_schmidt(2, outof)
    gram_schmidt(3, outof)
    z_step(3, 0)
    right_factors(outof)

    place = dp % 8
    line = dp // 8

    def part_of(j):
        return (
            pl.ds(pl.multiple_of((j % 4) * 8, 8), 8),
            pl.ds(pl.multiple_of((j // 4) * 384, 384), 384),
        )

    own_part = part_of(place)

    def e_copy(k):
        other = (place + k) % 8
        rows, lanes = part_of(other)
        return pltpu.make_async_remote_copy(
            src_ref=ql.at[rows, lanes], dst_ref=rq.at[k - 1],
            send_sem=e_send.at[k - 1], recv_sem=e_recv.at[k - 1],
            device_id=(line * 8 + other, mp), device_id_type=MESH,
        )

    def f_copy(k):
        return pltpu.make_async_remote_copy(
            src_ref=ry.at[line], dst_ref=ry.at[line],
            send_sem=f_send.at[k - 1], recv_sem=f_recv.at[k - 1],
            device_id=(((line + k) % 4) * 8 + place, mp), device_id_type=MESH,
        )

    def h_copy(k):
        own = qf.at[own_part[0], own_part[1]]
        return pltpu.make_async_remote_copy(
            src_ref=own, dst_ref=own,
            send_sem=h_send.at[k - 1], recv_sem=h_recv.at[k - 1],
            device_id=(line * 8 + (place + k) % 8, mp), device_id_type=MESH,
        )

    @pl.loop(1, 8)
    def _(k):
        e_copy(k).start()

    for h in (0, 1):
        @pl.loop(0, 3)
        def _(j):
            lanes = pl.ds(pl.multiple_of(j * 384, 384), 384)
            rows = pl.ds(pl.multiple_of(h * HALF + j * 384, 384), 384)
            by_row = jnp.transpose(ff[h, :, lanes])
            pt[rows, :] = by_row
            high, low = split(by_row)
            pc[rows, 0:128] = high
            pc[rows, 128:256] = high
            pc[rows, 256:384] = low

    @pl.loop(1, 8)
    def _(k):
        e_copy(k).wait_recv()

    ry[line] = ql[own_part[0], own_part[1]] + jnp.sum(rq[...], axis=0)

    @pl.loop(1, 4)
    def _(k):
        f_copy(k).start()

    z_step(4, 1)

    @pl.loop(1, 4)
    def _(k):
        f_copy(k).wait_recv()

    qf[own_part[0], own_part[1]] = (ry[0] + ry[1] + ry[2] + ry[3]) * (1.0 / N_DP)

    @pl.loop(1, 8)
    def _(k):
        h_copy(k).start()

    mine = jnp.transpose(pt[pl.ds(pl.multiple_of(dp * ROWS_P, 8), ROWS_P), :])
    for b, ref in enumerate((wide_p.at[0], narrow_p.at[0], narrow_p.at[1], wide_p.at[1])):
        ref[0] = mine[b * RANK:(b + 1) * RANK]

    @pl.loop(1, 8)
    def _(k):
        h_copy(k).wait_recv()

    for b, (at, width) in enumerate(COLS):
        q = qf[:, at:at + width]
        (wide_q, narrow_q)[width == 128][(0, 0, 1, 1)[b]] = q
        high, low = split(q)
        qbd[b * RANK:(b + 1) * RANK, at:at + width] = high
        qbd[128 + b * RANK:128 + (b + 1) * RANK, at:at + width] = low
        qbd[256 + b * RANK:256 + (b + 1) * RANK, at:at + width] = high

    z_step(4, 0)

    @pl.loop(0, 9)
    def _(j):
        rows = pl.ds(pl.multiple_of(j * 256, 256), 256)
        low_rank = dot(pc[rows, :], qbd[...])
        new = (sh[rows, :].astype(F32) + sl[rows, :].astype(F32) - low_rank).astype(BF16)
        for b, ref in enumerate((wide_new, narrow_new, narrow_new, wide_new)):
            at, width = COLS[b]
            ref[0, (0, 0, 1, 1)[b], rows, :] = new[:, at:at + width]


    for way in (0, 1):
        for role in (0, 1):
            z_hop(way, 4, role)[0].wait_recv()
    own = pl.ds(pl.multiple_of(mp * SHARE, SHARE), SHARE)
    input_grad[...] = (pg[own, :] + rr[0, 3] + rr[1, 3]).astype(BF16)

    drain_ring(x_hop)
    drain_ring(y_hop)
    for way in (0, 1):
        for step in (1, 2, 3, 4):
            for role in (0, 1):
                if (step, role) != (1, 1):
                    z_hop(way, step, role)[0].wait_send()

    @pl.loop(1, 8)
    def _(k):
        e_copy(k).wait_send()
        h_copy(k).wait_send()

    @pl.loop(1, 4)
    def _(k):
        f_copy(k).wait_send()


def hand_out(*refs):
    sources, targets, sem = refs[:7], refs[7:14], refs[14]
    copies = [pltpu.make_async_copy(a, b, sem.at[i]) for i, (a, b) in enumerate(zip(sources, targets))]
    for copy in copies:
        copy.start()
    for copy in copies:
        copy.wait()


def on_device(*args):
    sems = pltpu.SemaphoreType.DMA
    vmem = pltpu.VMEM
    args = args[:9] + tuple(jnp.swapaxes(a, 1, 2) for a in args[9:])
    shapes = (
        ((SHARE, D), BF16),
        ((2, 1, RANK, ROWS_P), F32),
        ((2, 1, RANK, ROWS_P), F32),
        ((2, RANK, 256), F32),
        ((2, RANK, 128), F32),
        ((1, 2, D, 256), BF16),
        ((1, 2, D, 128), BF16),
    )
    outs = pl.pallas_call(
        kernel,
        out_shape=tuple(pltpu.VMEM(shape, dtype) for shape, dtype in shapes),
        in_specs=[pl.BlockSpec(memory_space=pltpu.HBM)] * 11,
        out_specs=tuple([pl.BlockSpec(memory_space=pltpu.VMEM)] * 7),
        scratch_shapes=[
            vmem((TOK, D), BF16),
            vmem((TOK, D), BF16),
            vmem((TOK, ALL), BF16),
            vmem((D, INTO), BF16),
            vmem((D, ALL), BF16),
            vmem((2, RANK, 256), F32),
            vmem((2, RANK, 128), F32),
            vmem((2 * RANK, ALL), BF16),
            vmem((192, TOK), BF16),
            vmem((64, TOK), BF16),
            vmem((TOK, D), F32),
            vmem((2, 4, SHARE, D), F32),
            vmem((D, ALL), BF16),
            vmem((D, ALL), BF16),
            vmem((2, 128, HALF), F32),
            vmem((128, HALF), F32),
            vmem((CHIPS - 1, 8, HALF), F32),
            vmem((CHIPS - 1, 8, 384), F32),
            vmem((2, 128, HALF), F32),
            vmem((2, 32, HALF), F32),
            vmem((256, D), BF16),
            vmem((D, 128), F32),
            vmem((D, 384), BF16),
            vmem((RANK, ALL), F32),
            vmem((7, 8, 384), F32),
            vmem((4, 8, 384), F32),
            vmem((RANK, ALL), F32),
            vmem((384, ALL), BF16),
            sems((15,)),
            sems((2, 4, 4)), sems((2, 4, 4)),
            sems((2, 4, 4)), sems((2, 4, 4)),
            sems((2, 4, 2)), sems((2, 4, 2)),
            sems((2,)), sems((2,)),
            sems((2, CHIPS - 1)), sems((2, CHIPS - 1)),
            sems((2, CHIPS - 1)), sems((2, CHIPS - 1)),
            sems((2,)), sems((2,)),
            sems((7,)), sems((7,)),
            sems((3,)), sems((3,)),
            sems((7,)), sems((7,)),
        ],
        compiler_params=pltpu.CompilerParams(
            collective_id=0, has_side_effects=True, vmem_limit_bytes=59 * 1024 * 1024
        ),
    )(*args)
    outs = pl.pallas_call(
        hand_out,
        out_shape=tuple(jax.ShapeDtypeStruct(shape, dtype) for shape, dtype in shapes),
        in_specs=[pl.BlockSpec(memory_space=pltpu.VMEM)] * 7,
        out_specs=tuple([pl.BlockSpec(memory_space=pl.ANY)] * 7),
        scratch_shapes=[sems((7,))],
        compiler_params=pltpu.CompilerParams(vmem_limit_bytes=16 * 1024 * 1024),
    )(*outs)
    turned = [jnp.swapaxes(a, -1, -2) for a in outs[1:5]]
    return (outs[0], *turned, *outs[5:])


def solution(mesh):
    return jax.shard_map(
        on_device,
        mesh=mesh,
        in_specs=(
            P(("dp", "mp"), None),
            P(("dp", "mp"), None),
            P("dp", "mp"),
            P("dp", "mp"),
            P(None, "dp", "mp"),
            P(None, "mp"),
            P(None, None, "mp"),
            P("dp", None, None, "mp"),
            P("dp", None, None, "mp"),
            P(None, "mp", None),
            P(None, "mp", None),
        ),
        out_specs=(
            P(("dp", "mp"), None),
            P(None, "mp", "dp", None),
            P(None, "mp", "dp", None),
            P(None, "mp", None),
            P(None, "mp", None),
            P("dp", None, None, "mp"),
            P("dp", None, None, "mp"),
        ),
        check_vma=False,
    )
```

```python
import jax
import jax.numpy as jnp
from jax import lax
from jax.experimental import pallas as pl
from jax.experimental.pallas import tpu as pltpu
from jax.sharding import PartitionSpec as P

MESH = pl.DeviceIdType.MESH
F32 = jnp.float32
BF16 = jnp.bfloat16

D = 2304
HALF = D // 2
TOK = 512
SHARE = 64
PART = SHARE // 2
FINE = SHARE // 4
RANK = 32
N_DP = 32
N_MP = 8
CHIPS = N_DP // 2
REDUCERS = 12
ROWS_P = D // N_DP
COLS = ((0, 256), (256, 128), (384, 128), (512, 256))
INTO = 512
NEAR = 1792
ALL = 768


def split(value):
    high = value.astype(BF16)
    return high, (value - high.astype(F32)).astype(BF16)


def dot(a, b, on_a=1, on_b=0):
    return lax.dot_general(a, b, (((on_a,), (on_b,)), ((), ())), preferred_element_type=F32)


def kernel(
    x_in, out_grad, context, query_grad, keyval_grad, query_weight, keyval_weight,
    wide_error, narrow_error, wide_start, narrow_start,
    input_grad, wide_p, narrow_p, wide_q, narrow_q, wide_new, narrow_new,
    xf, yf, gv, wv, ev, sw, sn, st, tx, ty, pg, rr, sh, sl,
    wn, cn, fl, ra, rbx, rby, ff, rowbuf, pb, pt, pc, ql, rq, ry, qf, qbd,
    load_sem, x_send, x_recv, y_send, y_recv, z_send, z_recv,
    n_send, n_recv, p_send, p_recv, m_send, m_recv,
    a_send, a_recv, b_send, b_recv, c_send, c_recv, d_send, d_recv,
    e_send, e_recv, f_send, f_recv, h_send, h_recv,
):
    dp = lax.axis_index("dp")
    mp = lax.axis_index("mp")
    core = dp % 2
    chip = dp // 2
    mate = dp + 1 - 2 * core
    ring = ((mp + 1) % N_MP, (mp + N_MP - 1) % N_MP)

    def along(way, steps):
        return (mp + steps) % N_MP if way == 0 else (mp + N_MP - steps) % N_MP

    loads = [
        (query_grad, gv.at[:, 0:256]),
        (keyval_grad.at[0], gv.at[:, 256:384]),
        (keyval_grad.at[1], gv.at[:, 384:512]),
        (query_weight, wv.at[:, 0:256]),
        (keyval_weight.at[0], wv.at[:, 256:384]),
        (keyval_weight.at[1], wv.at[:, 384:512]),
        (wide_start, sw),
        (narrow_start, sn),
        (wide_error.at[0, 0], ev.at[:, 0:256]),
        (narrow_error.at[0, 0], ev.at[:, 256:384]),
        (narrow_error.at[0, 1], ev.at[:, 384:512]),
        (wide_error.at[0, 1], ev.at[:, 512:768]),
        (context, gv.at[:, 512:768]),
        (x_in, xf.at[pl.ds(pl.multiple_of(mp * SHARE, SHARE), SHARE), :]),
        (out_grad, yf.at[pl.ds(pl.multiple_of(mp * SHARE, SHARE), SHARE), :]),
    ]
    loads = [pltpu.make_async_copy(a, b, load_sem.at[i]) for i, (a, b) in enumerate(loads)]
    for i in range(6):
        loads[i].start()

    barrier = pltpu.get_barrier_semaphore()
    for way in (0, 1):
        pl.semaphore_signal(barrier, inc=1, device_id=(dp, ring[way]), device_id_type=MESH)

    @pl.loop(1, CHIPS)
    def _(k):
        other = 2 * ((chip + k) % CHIPS) + core
        pl.semaphore_signal(barrier, inc=1, device_id=(other, mp), device_id_type=MESH)

    @pl.loop(0, 4)
    def _(k):
        other = (dp // 8) * 8 + 2 * k + 1 - core
        pl.semaphore_signal(barrier, inc=1, device_id=(other, mp), device_id_type=MESH)

    pl.semaphore_wait(barrier, 2 + (CHIPS - 1) + 4)

    def hop(own, full, send, recv, way, step, role):
        part = role if way == 0 else 3 - role
        owner = along(1 - way, step - 1)
        rows = pl.ds(pl.multiple_of(owner * SHARE + part * FINE, FINE), FINE)
        src = own.at[part * FINE:(part + 1) * FINE, :] if step == 1 else full.at[rows, :]
        return pltpu.make_async_remote_copy(
            src_ref=src, dst_ref=full.at[rows, :],
            send_sem=send.at[way, step - 1, role], recv_sem=recv.at[way, step - 1, role],
            device_id=(dp, ring[way]), device_id_type=MESH,
        )

    def x_hop(way, step, role):
        return hop(x_in, xf, x_send, x_recv, way, step, role)

    def y_hop(way, step, role):
        return hop(out_grad, yf, y_send, y_recv, way, step, role)

    def first(make, roles=(0, 1, 2, 3)):
        for role in roles:
            for way in (0, 1):
                make(way, 1, role).start()

    def forward(make, step, *roles):
        for role in roles:
            for way in (0, 1):
                make(way, step - 1, role).wait_recv()
                make(way, step, role).start()

    def finish_ring(make):
        for step, role in ((3, 2), (3, 3), (4, 0), (4, 1)):
            for way in (0, 1):
                make(way, step, role).wait_recv()

    def drain_ring(make):
        for way in (0, 1):
            for step in (1, 2, 3, 4):
                for role in (0, 1, 2, 3):
                    if step < 4 or role < 2:
                        make(way, step, role).wait_send()

    def z_hop(way, step, role):
        part = way if role == 0 else 1 - way
        dest = along(way, 5 - step)
        rows = pl.ds(pl.multiple_of(dest * SHARE + part * PART, PART), PART)
        here = slice(part * PART, (part + 1) * PART)
        if step == 1 + role:
            src = pg.at[rows, NEAR:]
            dst = rr.at[way, step - 1, here, NEAR:]
        else:
            src = rr.at[way, step - 2, here, :]
            dst = rr.at[way, step - 1, here, :]
        return pltpu.make_async_remote_copy(
            src_ref=src, dst_ref=dst,
            send_sem=z_send.at[way, step - 1, role], recv_sem=z_recv.at[way, step - 1, role],
            device_id=(dp, ring[way]), device_id_type=MESH,
        ), rows, here

    def z_first(step, role):
        for way in (0, 1):
            z_hop(way, step, role)[0].start()

    def z_step(step, role):
        for way in (0, 1):
            z_hop(way, step - 1, role)[0].wait_recv()
            copy, rows, here = z_hop(way, step, role)
            if step == 2 + role:
                rr[way, step - 2, here, NEAR:] += pg[rows, NEAR:]
                rr[way, step - 2, here, :NEAR] = pg[rows, :NEAR]
            else:
                rr[way, step - 2, here, :] += pg[rows, :]
            copy.start()

    x_rows = slice(0, 96)
    y_rows = slice(96, 128)

    def chunk(group, p):
        if group == 0:
            return pl.ds(pl.multiple_of(p * 8, 8), 8), pl.ds(0, HALF)
        return (
            pl.ds(pl.multiple_of(96 + (p // 3) * 8, 8), 8),
            pl.ds(pl.multiple_of((p % 3) * 384, 384), 384),
        )

    def a_copy(group):
        rows = (x_rows, y_rows)[group]
        return pltpu.make_async_remote_copy(
            src_ref=fl.at[1 - core, rows], dst_ref=ra.at[rows],
            send_sem=a_send.at[group], recv_sem=a_recv.at[group],
            device_id=(mate, mp), device_id_type=MESH,
        )

    def b_copy(group, k, other):
        rows, lanes = chunk(group, other)
        return pltpu.make_async_remote_copy(
            src_ref=fl.at[core, rows, lanes], dst_ref=(rbx, rby)[group].at[k - 1],
            send_sem=b_send.at[group, k - 1], recv_sem=b_recv.at[group, k - 1],
            device_id=(2 * other + core, mp), device_id_type=MESH,
        )

    def c_copy(group, k, other, source):
        rows, lanes = chunk(group, source)
        own = ff.at[core, rows, lanes]
        return pltpu.make_async_remote_copy(
            src_ref=own, dst_ref=own,
            send_sem=c_send.at[group, k - 1], recv_sem=c_recv.at[group, k - 1],
            device_id=(2 * other + core, mp), device_id_type=MESH,
        )

    def d_copy(group):
        own = ff.at[core, (x_rows, y_rows)[group]]
        return pltpu.make_async_remote_copy(
            src_ref=own, dst_ref=own, send_sem=d_send.at[group], recv_sem=d_recv.at[group],
            device_id=(mate, mp), device_id_type=MESH,
        )

    def to_reducers(group):
        rows = (x_rows, y_rows)[group]
        a_copy(group).wait_recv()
        fl[core, rows] += ra[rows]

        @pl.loop(1, CHIPS)
        def _(k):
            other = (chip + k) % CHIPS

            @pl.when(other < REDUCERS)
            def _():
                b_copy(group, k, other).start()

    def from_reducers(group):
        @pl.when(chip < REDUCERS)
        def _():
            @pl.loop(1, CHIPS)
            def _(k):
                b_copy(group, k, chip).wait_recv()

            rows, lanes = chunk(group, chip)
            ff[core, rows, lanes] = fl[core, rows, lanes] + jnp.sum((rbx, rby)[group][...], axis=0)

            @pl.loop(1, CHIPS)
            def _(k):
                c_copy(group, k, (chip + k) % CHIPS, chip).start()

    def to_mate(group):
        @pl.loop(1, CHIPS)
        def _(k):
            source = (chip + CHIPS - k) % CHIPS

            @pl.when(source < REDUCERS)
            def _():
                c_copy(group, k, chip, source).wait_recv()

        d_copy(group).start()

    def from_mate(group):
        a_copy(group).wait_send()

        @pl.loop(1, CHIPS)
        def _(k):
            other = (chip + k) % CHIPS

            @pl.when(other < REDUCERS)
            def _():
                b_copy(group, k, other).wait_send()

        @pl.when(chip < REDUCERS)
        def _():
            @pl.loop(1, CHIPS)
            def _(k):
                c_copy(group, k, (chip + k) % CHIPS, chip).wait_send()

        d_copy(group).wait()

    rows_each = NEAR // CHIPS
    half = pl.ds(pl.multiple_of(core * 256, 256), 256)
    share = pl.ds(pl.multiple_of(chip * rows_each, rows_each), rows_each)

    def feature_copy(way, role):
        part = way if role == 0 else 1 - way
        dest = along(way, 4 - role)
        rows = pl.ds(pl.multiple_of(dest * SHARE + part * PART, PART), PART)
        return pltpu.make_async_remote_copy(
            src_ref=gv.at[rows, 0:INTO], dst_ref=cn.at[way, role * PART:(role + 1) * PART, :],
            send_sem=n_send.at[way, role], recv_sem=n_recv.at[way, role],
            device_id=(dp, ring[way]), device_id_type=MESH,
        )

    def weight_copy(way):
        return pltpu.make_async_remote_copy(
            src_ref=wv.at[share, half], dst_ref=wn.at[way, share, half],
            send_sem=n_send.at[way, 2], recv_sem=n_recv.at[way, 2],
            device_id=(dp, ring[way]), device_id_type=MESH,
        )

    def plane_copy(way, k):
        own = wn.at[way, share, half]
        return pltpu.make_async_remote_copy(
            src_ref=own, dst_ref=own,
            send_sem=p_send.at[way, k - 1], recv_sem=p_recv.at[way, k - 1],
            device_id=(2 * ((chip + k) % CHIPS) + core, mp), device_id_type=MESH,
        )

    def mate_copy(way):
        own = wn.at[way, :, half]
        return pltpu.make_async_remote_copy(
            src_ref=own, dst_ref=own, send_sem=m_send.at[way], recv_sem=m_recv.at[way],
            device_id=(mate, mp), device_id_type=MESH,
        )

    def to_neighbours():
        for way in (0, 1):
            weight_copy(way).start()
        for way in (0, 1):
            for role in (0, 1):
                feature_copy(way, role).start()

    def weights_to_plane():
        for way in (0, 1):
            weight_copy(way).wait_recv()

        @pl.loop(1, CHIPS)
        def _(k):
            for way in (0, 1):
                plane_copy(way, k).start()

    def weights_to_mate():
        @pl.loop(1, CHIPS)
        def _(k):
            for way in (0, 1):
                plane_copy(way, k).wait_recv()

        for way in (0, 1):
            mate_copy(way).start()

    def add_neighbour_features():
        for way in (0, 1):
            mate_copy(way).wait_recv()
            for role in (0, 1):
                feature_copy(way, role).wait_recv()

        @pl.loop(0, NEAR // 256)
        def _(j):
            cols = pl.ds(pl.multiple_of(j * 256, 256), 256)
            for way in (0, 1):
                more = dot(cn[way], wn[way, cols, :], 1, 1)
                for role in (0, 1):
                    part = way if role == 0 else 1 - way
                    dest = along(way, 3 - role)
                    rows = pl.ds(pl.multiple_of(dest * SHARE + part * PART, PART), PART)
                    pg[rows, cols] += more[role * PART:(role + 1) * PART]

    def drain_neighbours():
        for way in (0, 1):
            weight_copy(way).wait_send()
            mate_copy(way).wait_send()
            for role in (0, 1):
                feature_copy(way, role).wait_send()

        @pl.loop(1, CHIPS)
        def _(k):
            for way in (0, 1):
                plane_copy(way, k).wait_send()

    first(x_hop)
    for copy in loads[6:]:
        copy.start()
    for i in range(6):
        loads[i].wait()
    to_neighbours()

    def partial_input_grad(start, stop):
        @pl.loop(start, stop)
        def _(j):
            cols = pl.ds(pl.multiple_of(j * 256, 256), 256)
            pg[:, cols] = dot(gv[:, 0:INTO], wv[cols, :], 1, 1)

    partial_input_grad(0, 3)
    forward(x_hop, 2, 0, 1)
    partial_input_grad(3, 6)
    forward(x_hop, 2, 2, 3)
    weights_to_plane()
    partial_input_grad(6, 9)
    forward(x_hop, 3, 0)

    for i in (6, 7):
        loads[i].wait()
    for b, (at, width) in enumerate(COLS):
        high, low = split(sw[0 if b == 0 else 1] if width == 256 else sn[b - 1])
        st[0:RANK, at:at + width] = high
        st[RANK:2 * RANK, at:at + width] = low
    loads[12].wait()
    for b, (at, width) in enumerate(COLS):
        t = dot(st[:, at:at + width], gv[:, at:at + width], 1, 1)
        high, low = split(t[:RANK] + t[RANK:])
        if b < 3:
            tx[b * RANK:(b + 1) * RANK, :] = high
            tx[96 + b * RANK:96 + (b + 1) * RANK, :] = low
        else:
            ty[0:RANK, :] = high
            ty[RANK:2 * RANK, :] = low
    qbd[...] = jnp.zeros_like(qbd)

    forward(x_hop, 3, 1)
    for i in (8, 9, 10, 11):
        loads[i].wait()

    def error_factors(start, stop):
        @pl.loop(start, stop)
        def _(j):
            rows = pl.ds(pl.multiple_of(j * 384, 384), 384)
            lanes = pl.ds(pl.multiple_of((j % 3) * 384, 384), 384)
            for b, (at, width) in enumerate(COLS):
                e = dot(st[:, at:at + width], ev[rows, at:at + width], 1, 1)
                fl[j // 3, b * RANK:(b + 1) * RANK, lanes] = e[:RANK] + e[RANK:]

    error_factors(0, 3)
    forward(x_hop, 3, 2)
    error_factors(3, 6)
    forward(x_hop, 3, 3)
    forward(x_hop, 4, 0, 1)
    first(y_hop)
    loads[13].wait()
    finish_ring(x_hop)

    @pl.loop(0, 6)
    def _(j):
        cols = pl.ds(pl.multiple_of(j * 384, 384), 384)
        lanes = pl.ds(pl.multiple_of((j % 3) * 384, 384), 384)
        f = dot(tx[...], xf[:, cols])
        fl[j // 3, 0:96, lanes] += f[:96] + f[96:]

    a_copy(0).start()

    def sums_into(start, stop):
        @pl.loop(start, stop)
        def _(j):
            rows = pl.ds(pl.multiple_of(j * 256, 256), 256)
            total = dot(xf[:, rows], gv[:, 0:INTO], 0, 0) + ev[rows, 0:INTO].astype(F32)
            high, low = split(total)
            sh[rows, 0:INTO] = high
            sl[rows, 0:INTO] = low

    forward(y_hop, 2, 0, 1, 2)
    forward(y_hop, 2, 3)
    weights_to_mate()
    sums_into(0, 3)
    to_reducers(0)
    forward(y_hop, 3, 0)
    sums_into(3, 6)
    forward(y_hop, 3, 1)
    sums_into(6, 9)
    forward(y_hop, 3, 2, 3)
    forward(y_hop, 4, 0, 1)
    from_reducers(0)
    add_neighbour_features()
    loads[14].wait()
    finish_ring(y_hop)
    z_first(1, 0)

    @pl.loop(0, 6)
    def _(j):
        cols = pl.ds(pl.multiple_of(j * 384, 384), 384)
        lanes = pl.ds(pl.multiple_of((j % 3) * 384, 384), 384)
        f = dot(ty[...], yf[:, cols])
        fl[j // 3, 96:128, lanes] += f[:RANK] + f[RANK:]

    a_copy(1).start()
    z_first(2, 1)
    to_mate(0)

    def gram_schmidt(block, which):
        @pl.loop(0, 8)
        def _(i):
            norms = {}
            for b in which:
                row = [ff[h, pl.ds(b * RANK + block * 8 + i, 1), :] for h in (0, 1)]
                for h in (0, 1):
                    rowbuf[h, b * 8:b * 8 + 8, :] = jnp.broadcast_to(row[h], (8, HALF))
                norms[b] = jnp.sum(row[0] * row[0] + row[1] * row[1], axis=1, keepdims=True)
            later = lax.broadcasted_iota(jnp.int32, (8, 1), 0) > i
            scales = {}
            for b in which:
                for t in range(block, 4):
                    at = slice(b * RANK + t * 8, b * RANK + t * 8 + 8)
                    r = slice(b * 8, b * 8 + 8)
                    dots = jnp.sum(
                        ff[0, at, :] * rowbuf[0, r, :] + ff[1, at, :] * rowbuf[1, r, :],
                        axis=1, keepdims=True,
                    )
                    scale = dots / norms[b]
                    scales[b, t] = jnp.where(later, scale, 0.0) if t == block else scale
            for b in which:
                for t in range(block, 4):
                    at = slice(b * RANK + t * 8, b * RANK + t * 8 + 8)
                    for h in (0, 1):
                        ff[h, at, :] -= scales[b, t] * rowbuf[h, b * 8:b * 8 + 8, :]

    def right_factors(which):
        for b in which:
            at = slice(b * RANK, (b + 1) * RANK)
            squares = jnp.sum(
                ff[0, at, :] * ff[0, at, :] + ff[1, at, :] * ff[1, at, :], axis=1, keepdims=True
            )
            size = jnp.sqrt(squares)
            for h in (0, 1):
                unit = ff[h, at, :] / size
                ff[h, at, :] = unit
                high, low = split(unit)
                pb[2 * b * RANK:(2 * b + 1) * RANK, h * HALF:(h + 1) * HALF] = high
                pb[(2 * b + 1) * RANK:(2 * b + 2) * RANK, h * HALF:(h + 1) * HALF] = low
        for b in which:
            at, width = COLS[b]
            both = dot(pb[2 * b * RANK:(2 * b + 2) * RANK, :], sh[:, at:at + width])
            rest = dot(pb[2 * b * RANK:(2 * b + 1) * RANK, :], sl[:, at:at + width])
            ql[:, at:at + width] = both[:RANK] + both[RANK:] + rest

    into = (0, 1, 2)
    outof = (3,)

    @pl.loop(0, 9)
    def _(j):
        rows = pl.ds(pl.multiple_of(j * 256, 256), 256)
        total = dot(yf[:, rows], gv[:, INTO:ALL], 0, 0) + ev[rows, INTO:ALL].astype(F32)
        high, low = split(total)
        sh[rows, INTO:ALL] = high
        sl[rows, INTO:ALL] = low

    z_step(2, 0)
    to_reducers(1)
    z_step(3, 1)
    from_mate(0)
    gram_schmidt(0, into)
    from_reducers(1)
    gram_schmidt(1, into)
    gram_schmidt(2, into)
    gram_schmidt(3, into)
    to_mate(1)
    right_factors(into)
    from_mate(1)
    gram_schmidt(0, outof)
    gram_schmidt(1, outof)
    z_step(3, 0)
    gram_schmidt(2, outof)
    gram_schmidt(3, outof)
    right_factors(outof)

    place = dp % 8
    line = dp // 8

    def part_of(j):
        return (
            pl.ds(pl.multiple_of((j % 4) * 8, 8), 8),
            pl.ds(pl.multiple_of((j // 4) * 384, 384), 384),
        )

    own_part = part_of(place)

    def e_copy(k):
        other = (place + k) % 8
        rows, lanes = part_of(other)
        return pltpu.make_async_remote_copy(
            src_ref=ql.at[rows, lanes], dst_ref=rq.at[k - 1],
            send_sem=e_send.at[k - 1], recv_sem=e_recv.at[k - 1],
            device_id=(line * 8 + other, mp), device_id_type=MESH,
        )

    def f_copy(k):
        return pltpu.make_async_remote_copy(
            src_ref=ry.at[line], dst_ref=ry.at[line],
            send_sem=f_send.at[k - 1], recv_sem=f_recv.at[k - 1],
            device_id=(((line + k) % 4) * 8 + place, mp), device_id_type=MESH,
        )

    def h_copy(k):
        own = qf.at[own_part[0], own_part[1]]
        return pltpu.make_async_remote_copy(
            src_ref=own, dst_ref=own,
            send_sem=h_send.at[k - 1], recv_sem=h_recv.at[k - 1],
            device_id=(line * 8 + (place + k) % 8, mp), device_id_type=MESH,
        )

    @pl.loop(1, 8)
    def _(k):
        e_copy(k).start()

    def left_by_rows(start, stop):
        @pl.loop(start, stop)
        def _(j):
            lanes = pl.ds(pl.multiple_of((j % 3) * 384, 384), 384)
            rows = pl.ds(pl.multiple_of(j * 384, 384), 384)
            by_row = jnp.transpose(ff[j // 3, :, lanes])
            pt[rows, :] = by_row
            high, low = split(by_row)
            pc[rows, 0:128] = high
            pc[rows, 128:256] = high
            pc[rows, 256:384] = low

    z_step(4, 1)
    left_by_rows(0, 2)

    @pl.loop(1, 8)
    def _(k):
        e_copy(k).wait_recv()

    ry[line] = ql[own_part[0], own_part[1]] + jnp.sum(rq[...], axis=0)

    @pl.loop(1, 4)
    def _(k):
        f_copy(k).start()

    left_by_rows(2, 4)

    @pl.loop(1, 4)
    def _(k):
        f_copy(k).wait_recv()

    qf[own_part[0], own_part[1]] = (ry[0] + ry[1] + ry[2] + ry[3]) * (1.0 / N_DP)

    @pl.loop(1, 8)
    def _(k):
        h_copy(k).start()

    z_step(4, 0)
    left_by_rows(4, 6)
    mine = jnp.transpose(pt[pl.ds(pl.multiple_of(dp * ROWS_P, 8), ROWS_P), :])
    for b, ref in enumerate((wide_p.at[0], narrow_p.at[0], narrow_p.at[1], wide_p.at[1])):
        ref[0] = mine[b * RANK:(b + 1) * RANK]

    @pl.loop(1, 8)
    def _(k):
        h_copy(k).wait_recv()

    for b, (at, width) in enumerate(COLS):
        q = qf[:, at:at + width]
        (wide_q, narrow_q)[width == 128][(0, 0, 1, 1)[b]] = q
        high, low = split(q)
        qbd[b * RANK:(b + 1) * RANK, at:at + width] = high
        qbd[128 + b * RANK:128 + (b + 1) * RANK, at:at + width] = low
        qbd[256 + b * RANK:256 + (b + 1) * RANK, at:at + width] = high

    @pl.loop(0, 9)
    def _(j):
        rows = pl.ds(pl.multiple_of(j * 256, 256), 256)
        low_rank = dot(pc[rows, :], qbd[...])
        new = (sh[rows, :].astype(F32) + sl[rows, :].astype(F32) - low_rank).astype(BF16)
        for b, ref in enumerate((wide_new, narrow_new, narrow_new, wide_new)):
            at, width = COLS[b]
            ref[0, (0, 0, 1, 1)[b], rows, :] = new[:, at:at + width]


    for way in (0, 1):
        for role in (0, 1):
            z_hop(way, 4, role)[0].wait_recv()
    own = pl.ds(pl.multiple_of(mp * SHARE, SHARE), SHARE)
    input_grad[...] = (pg[own, :] + rr[0, 3] + rr[1, 3]).astype(BF16)

    drain_neighbours()
    drain_ring(x_hop)
    drain_ring(y_hop)
    for way in (0, 1):
        for step in (1, 2, 3, 4):
            for role in (0, 1):
                if (step, role) != (1, 1):
                    z_hop(way, step, role)[0].wait_send()

    @pl.loop(1, 8)
    def _(k):
        e_copy(k).wait_send()
        h_copy(k).wait_send()

    @pl.loop(1, 4)
    def _(k):
        f_copy(k).wait_send()


def hand_out(*refs):
    sources, targets, sem = refs[:7], refs[7:14], refs[14]
    copies = [pltpu.make_async_copy(a, b, sem.at[i]) for i, (a, b) in enumerate(zip(sources, targets))]
    for copy in copies:
        copy.start()
    for copy in copies:
        copy.wait()


def on_device(*args):
    sems = pltpu.SemaphoreType.DMA
    vmem = pltpu.VMEM
    args = args[:9] + tuple(jnp.swapaxes(a, 1, 2) for a in args[9:])
    shapes = (
        ((SHARE, D), BF16),
        ((2, 1, RANK, ROWS_P), F32),
        ((2, 1, RANK, ROWS_P), F32),
        ((2, RANK, 256), F32),
        ((2, RANK, 128), F32),
        ((1, 2, D, 256), BF16),
        ((1, 2, D, 128), BF16),
    )
    outs = pl.pallas_call(
        kernel,
        out_shape=tuple(pltpu.VMEM(shape, dtype) for shape, dtype in shapes),
        in_specs=[pl.BlockSpec(memory_space=pltpu.HBM)] * 11,
        out_specs=tuple([pl.BlockSpec(memory_space=pltpu.VMEM)] * 7),
        scratch_shapes=[
            vmem((TOK, D), BF16),
            vmem((TOK, D), BF16),
            vmem((TOK, ALL), BF16),
            vmem((D, INTO), BF16),
            vmem((D, ALL), BF16),
            vmem((2, RANK, 256), F32),
            vmem((2, RANK, 128), F32),
            vmem((2 * RANK, ALL), BF16),
            vmem((192, TOK), BF16),
            vmem((64, TOK), BF16),
            vmem((TOK, D), F32),
            vmem((2, 4, SHARE, D), F32),
            vmem((D, ALL), BF16),
            vmem((D, ALL), BF16),
            vmem((2, NEAR, INTO), BF16),
            vmem((2, SHARE, INTO), BF16),
            vmem((2, 128, HALF), F32),
            vmem((128, HALF), F32),
            vmem((CHIPS - 1, 8, HALF), F32),
            vmem((CHIPS - 1, 8, 384), F32),
            vmem((2, 128, HALF), F32),
            vmem((2, 32, HALF), F32),
            vmem((256, D), BF16),
            vmem((D, 128), F32),
            vmem((D, 384), BF16),
            vmem((RANK, ALL), F32),
            vmem((7, 8, 384), F32),
            vmem((4, 8, 384), F32),
            vmem((RANK, ALL), F32),
            vmem((384, ALL), BF16),
            sems((15,)),
            sems((2, 4, 4)), sems((2, 4, 4)),
            sems((2, 4, 4)), sems((2, 4, 4)),
            sems((2, 4, 2)), sems((2, 4, 2)),
            sems((2, 3)), sems((2, 3)),
            sems((2, CHIPS - 1)), sems((2, CHIPS - 1)),
            sems((2,)), sems((2,)),
            sems((2,)), sems((2,)),
            sems((2, CHIPS - 1)), sems((2, CHIPS - 1)),
            sems((2, CHIPS - 1)), sems((2, CHIPS - 1)),
            sems((2,)), sems((2,)),
            sems((7,)), sems((7,)),
            sems((3,)), sems((3,)),
            sems((7,)), sems((7,)),
        ],
        compiler_params=pltpu.CompilerParams(
            collective_id=0, has_side_effects=True, vmem_limit_bytes=59 * 1024 * 1024
        ),
    )(*args)
    outs = pl.pallas_call(
        hand_out,
        out_shape=tuple(jax.ShapeDtypeStruct(shape, dtype) for shape, dtype in shapes),
        in_specs=[pl.BlockSpec(memory_space=pltpu.VMEM)] * 7,
        out_specs=tuple([pl.BlockSpec(memory_space=pl.ANY)] * 7),
        scratch_shapes=[sems((7,))],
        compiler_params=pltpu.CompilerParams(vmem_limit_bytes=16 * 1024 * 1024),
    )(*outs)
    turned = [jnp.swapaxes(a, -1, -2) for a in outs[1:5]]
    return (outs[0], *turned, *outs[5:])


def solution(mesh):
    return jax.shard_map(
        on_device,
        mesh=mesh,
        in_specs=(
            P(("dp", "mp"), None),
            P(("dp", "mp"), None),
            P("dp", "mp"),
            P("dp", "mp"),
            P(None, "dp", "mp"),
            P(None, "mp"),
            P(None, None, "mp"),
            P("dp", None, None, "mp"),
            P("dp", None, None, "mp"),
            P(None, "mp", None),
            P(None, "mp", None),
        ),
        out_specs=(
            P(("dp", "mp"), None),
            P(None, "mp", "dp", None),
            P(None, "mp", "dp", None),
            P(None, "mp", None),
            P(None, "mp", None),
            P("dp", None, None, "mp"),
            P("dp", None, None, "mp"),
        ),
        check_vma=False,
    )
```

```python
import jax
import jax.numpy as jnp
from jax import lax
from jax.experimental import pallas as pl
from jax.experimental.pallas import tpu as pltpu
from jax.sharding import PartitionSpec as P

MESH = pl.DeviceIdType.MESH
F32 = jnp.float32
BF16 = jnp.bfloat16

D = 2304
HALF = D // 2
TOK = 512
SHARE = 64
PART = SHARE // 2
FINE = SHARE // 4
RANK = 32
N_DP = 32
N_MP = 8
CHIPS = N_DP // 2
REDUCERS = 12
ROWS_P = D // N_DP
COLS = ((0, 256), (256, 128), (384, 128), (512, 256))
INTO = 512
NEAR = 1792
ALL = 768


def split(value):
    high = value.astype(BF16)
    return high, (value - high.astype(F32)).astype(BF16)


def dot(a, b, on_a=1, on_b=0):
    return lax.dot_general(a, b, (((on_a,), (on_b,)), ((), ())), preferred_element_type=F32)


def kernel(
    x_in, out_grad, context, query_grad, keyval_grad, query_weight, keyval_weight,
    wide_error, narrow_error, wide_start, narrow_start,
    input_grad, wide_p, narrow_p, wide_q, narrow_q, wide_new, narrow_new,
    xf, yf, gv, wv, ev, sw, sn, st, tx, ty, pg, rr, sh, sl,
    wn, cn, fl, ra, rbx, rby, ff, rowbuf, pb, pt, pc, ql, rq, ry, qf, qbd,
    load_sem, x_send, x_recv, y_send, y_recv, z_send, z_recv,
    n_send, n_recv, p_send, p_recv, m_send, m_recv,
    a_send, a_recv, b_send, b_recv, c_send, c_recv, d_send, d_recv,
    e_send, e_recv, f_send, f_recv, h_send, h_recv,
):
    dp = lax.axis_index("dp")
    mp = lax.axis_index("mp")
    core = dp % 2
    chip = dp // 2
    mate = dp + 1 - 2 * core
    ring = ((mp + 1) % N_MP, (mp + N_MP - 1) % N_MP)

    def along(way, steps):
        return (mp + steps) % N_MP if way == 0 else (mp + N_MP - steps) % N_MP

    loads = [
        (query_grad, gv.at[:, 0:256]),
        (keyval_grad.at[0], gv.at[:, 256:384]),
        (keyval_grad.at[1], gv.at[:, 384:512]),
        (query_weight, wv.at[:, 0:256]),
        (keyval_weight.at[0], wv.at[:, 256:384]),
        (keyval_weight.at[1], wv.at[:, 384:512]),
        (wide_start, sw),
        (narrow_start, sn),
        (wide_error.at[0, 0], ev.at[:, 0:256]),
        (narrow_error.at[0, 0], ev.at[:, 256:384]),
        (narrow_error.at[0, 1], ev.at[:, 384:512]),
        (wide_error.at[0, 1], ev.at[:, 512:768]),
        (context, gv.at[:, 512:768]),
        (x_in, xf.at[pl.ds(pl.multiple_of(mp * SHARE, SHARE), SHARE), :]),
        (out_grad, yf.at[pl.ds(pl.multiple_of(mp * SHARE, SHARE), SHARE), :]),
    ]
    loads = [pltpu.make_async_copy(a, b, load_sem.at[i]) for i, (a, b) in enumerate(loads)]
    for i in range(6):
        loads[i].start()

    barrier = pltpu.get_barrier_semaphore()
    for way in (0, 1):
        pl.semaphore_signal(barrier, inc=1, device_id=(dp, ring[way]), device_id_type=MESH)

    @pl.loop(1, CHIPS)
    def _(k):
        other = 2 * ((chip + k) % CHIPS) + core
        pl.semaphore_signal(barrier, inc=1, device_id=(other, mp), device_id_type=MESH)

    @pl.loop(0, 4)
    def _(k):
        other = (dp // 8) * 8 + 2 * k + 1 - core
        pl.semaphore_signal(barrier, inc=1, device_id=(other, mp), device_id_type=MESH)

    pl.semaphore_wait(barrier, 2 + (CHIPS - 1) + 4)

    def hop(own, full, send, recv, way, step, role):
        part = role if way == 0 else 3 - role
        owner = along(1 - way, step - 1)
        rows = pl.ds(pl.multiple_of(owner * SHARE + part * FINE, FINE), FINE)
        src = own.at[part * FINE:(part + 1) * FINE, :] if step == 1 else full.at[rows, :]
        return pltpu.make_async_remote_copy(
            src_ref=src, dst_ref=full.at[rows, :],
            send_sem=send.at[way, step - 1, role], recv_sem=recv.at[way, step - 1, role],
            device_id=(dp, ring[way]), device_id_type=MESH,
        )

    def x_hop(way, step, role):
        return hop(x_in, xf, x_send, x_recv, way, step, role)

    def y_hop(way, step, role):
        return hop(out_grad, yf, y_send, y_recv, way, step, role)

    def first(make, roles=(0, 1, 2, 3)):
        for role in roles:
            for way in (0, 1):
                make(way, 1, role).start()

    def forward(make, step, *roles):
        for role in roles:
            for way in (0, 1):
                make(way, step - 1, role).wait_recv()
                make(way, step, role).start()

    def finish_ring(make):
        for step, role in ((3, 2), (3, 3), (4, 0), (4, 1)):
            for way in (0, 1):
                make(way, step, role).wait_recv()

    def drain_ring(make):
        for way in (0, 1):
            for step in (1, 2, 3, 4):
                for role in (0, 1, 2, 3):
                    if step < 4 or role < 2:
                        make(way, step, role).wait_send()

    def z_hop(way, step, role):
        part = way if role == 0 else 1 - way
        dest = along(way, 5 - step)
        rows = pl.ds(pl.multiple_of(dest * SHARE + part * PART, PART), PART)
        here = slice(part * PART, (part + 1) * PART)
        if step == 1 + role:
            src = pg.at[rows, NEAR:]
            dst = rr.at[way, step - 1, here, NEAR:]
        else:
            src = rr.at[way, step - 2, here, :]
            dst = rr.at[way, step - 1, here, :]
        return pltpu.make_async_remote_copy(
            src_ref=src, dst_ref=dst,
            send_sem=z_send.at[way, step - 1, role], recv_sem=z_recv.at[way, step - 1, role],
            device_id=(dp, ring[way]), device_id_type=MESH,
        ), rows, here

    def z_first(step, role):
        for way in (0, 1):
            z_hop(way, step, role)[0].start()

    def z_step(step, role):
        for way in (0, 1):
            z_hop(way, step - 1, role)[0].wait_recv()
            copy, rows, here = z_hop(way, step, role)
            if step == 2 + role:
                rr[way, step - 2, here, NEAR:] += pg[rows, NEAR:]
                rr[way, step - 2, here, :NEAR] = pg[rows, :NEAR]
            else:
                rr[way, step - 2, here, :] += pg[rows, :]
            copy.start()

    x_rows = slice(0, 96)
    y_rows = slice(96, 128)

    def chunk(group, p):
        if group == 0:
            return pl.ds(pl.multiple_of(p * 8, 8), 8), pl.ds(0, HALF)
        return (
            pl.ds(pl.multiple_of(96 + (p // 3) * 8, 8), 8),
            pl.ds(pl.multiple_of((p % 3) * 384, 384), 384),
        )

    def a_copy(group):
        rows = (x_rows, y_rows)[group]
        return pltpu.make_async_remote_copy(
            src_ref=fl.at[1 - core, rows], dst_ref=ra.at[rows],
            send_sem=a_send.at[group], recv_sem=a_recv.at[group],
            device_id=(mate, mp), device_id_type=MESH,
        )

    def b_copy(group, k, other):
        rows, lanes = chunk(group, other)
        return pltpu.make_async_remote_copy(
            src_ref=fl.at[core, rows, lanes], dst_ref=(rbx, rby)[group].at[k - 1],
            send_sem=b_send.at[group, k - 1], recv_sem=b_recv.at[group, k - 1],
            device_id=(2 * other + core, mp), device_id_type=MESH,
        )

    def c_copy(group, k, other, source):
        rows, lanes = chunk(group, source)
        own = ff.at[core, rows, lanes]
        return pltpu.make_async_remote_copy(
            src_ref=own, dst_ref=own,
            send_sem=c_send.at[group, k - 1], recv_sem=c_recv.at[group, k - 1],
            device_id=(2 * other + core, mp), device_id_type=MESH,
        )

    def d_copy(group):
        own = ff.at[core, (x_rows, y_rows)[group]]
        return pltpu.make_async_remote_copy(
            src_ref=own, dst_ref=own, send_sem=d_send.at[group], recv_sem=d_recv.at[group],
            device_id=(mate, mp), device_id_type=MESH,
        )

    def to_reducers(group):
        rows = (x_rows, y_rows)[group]
        a_copy(group).wait_recv()
        fl[core, rows] += ra[rows]

        @pl.loop(1, CHIPS)
        def _(k):
            other = (chip + k) % CHIPS

            @pl.when(other < REDUCERS)
            def _():
                b_copy(group, k, other).start()

    def from_reducers(group):
        @pl.when(chip < REDUCERS)
        def _():
            @pl.loop(1, CHIPS)
            def _(k):
                b_copy(group, k, chip).wait_recv()

            rows, lanes = chunk(group, chip)
            ff[core, rows, lanes] = fl[core, rows, lanes] + jnp.sum((rbx, rby)[group][...], axis=0)

            @pl.loop(1, CHIPS)
            def _(k):
                c_copy(group, k, (chip + k) % CHIPS, chip).start()

    def to_mate(group):
        @pl.loop(1, CHIPS)
        def _(k):
            source = (chip + CHIPS - k) % CHIPS

            @pl.when(source < REDUCERS)
            def _():
                c_copy(group, k, chip, source).wait_recv()

        d_copy(group).start()

    def from_mate(group):
        a_copy(group).wait_send()

        @pl.loop(1, CHIPS)
        def _(k):
            other = (chip + k) % CHIPS

            @pl.when(other < REDUCERS)
            def _():
                b_copy(group, k, other).wait_send()

        @pl.when(chip < REDUCERS)
        def _():
            @pl.loop(1, CHIPS)
            def _(k):
                c_copy(group, k, (chip + k) % CHIPS, chip).wait_send()

        d_copy(group).wait()

    rows_each = NEAR // CHIPS
    half = pl.ds(pl.multiple_of(core * 256, 256), 256)
    share = pl.ds(pl.multiple_of(chip * rows_each, rows_each), rows_each)

    def feature_copy(way, role):
        part = way if role == 0 else 1 - way
        dest = along(way, 4 - role)
        rows = pl.ds(pl.multiple_of(dest * SHARE + part * PART, PART), PART)
        return pltpu.make_async_remote_copy(
            src_ref=gv.at[rows, 0:INTO], dst_ref=cn.at[way, role * PART:(role + 1) * PART, :],
            send_sem=n_send.at[way, role], recv_sem=n_recv.at[way, role],
            device_id=(dp, ring[way]), device_id_type=MESH,
        )

    def weight_copy(way):
        return pltpu.make_async_remote_copy(
            src_ref=wv.at[share, half], dst_ref=wn.at[way, share, half],
            send_sem=n_send.at[way, 2], recv_sem=n_recv.at[way, 2],
            device_id=(dp, ring[way]), device_id_type=MESH,
        )

    def plane_copy(way, k):
        own = wn.at[way, share, half]
        return pltpu.make_async_remote_copy(
            src_ref=own, dst_ref=own,
            send_sem=p_send.at[way, k - 1], recv_sem=p_recv.at[way, k - 1],
            device_id=(2 * ((chip + k) % CHIPS) + core, mp), device_id_type=MESH,
        )

    def mate_copy(way):
        own = wn.at[way, :, half]
        return pltpu.make_async_remote_copy(
            src_ref=own, dst_ref=own, send_sem=m_send.at[way], recv_sem=m_recv.at[way],
            device_id=(mate, mp), device_id_type=MESH,
        )

    def to_neighbours():
        for way in (0, 1):
            weight_copy(way).start()
        for way in (0, 1):
            for role in (0, 1):
                feature_copy(way, role).start()

    def weights_to_plane():
        for way in (0, 1):
            weight_copy(way).wait_recv()

        @pl.loop(1, CHIPS)
        def _(k):
            for way in (0, 1):
                plane_copy(way, k).start()

    def weights_to_mate():
        @pl.loop(1, CHIPS)
        def _(k):
            for way in (0, 1):
                plane_copy(way, k).wait_recv()

        for way in (0, 1):
            mate_copy(way).start()

    def add_neighbour_features():
        for way in (0, 1):
            mate_copy(way).wait_recv()
            for role in (0, 1):
                feature_copy(way, role).wait_recv()

        @pl.loop(0, NEAR // 256)
        def _(j):
            cols = pl.ds(pl.multiple_of(j * 256, 256), 256)
            for way in (0, 1):
                more = dot(cn[way], wn[way, cols, :], 1, 1)
                for role in (0, 1):
                    part = way if role == 0 else 1 - way
                    dest = along(way, 3 - role)
                    rows = pl.ds(pl.multiple_of(dest * SHARE + part * PART, PART), PART)
                    pg[rows, cols] += more[role * PART:(role + 1) * PART]

    def drain_neighbours():
        for way in (0, 1):
            weight_copy(way).wait_send()
            mate_copy(way).wait_send()
            for role in (0, 1):
                feature_copy(way, role).wait_send()

        @pl.loop(1, CHIPS)
        def _(k):
            for way in (0, 1):
                plane_copy(way, k).wait_send()

    first(x_hop)
    for copy in loads[6:]:
        copy.start()
    for i in range(6):
        loads[i].wait()
    to_neighbours()

    def partial_input_grad(start, stop):
        @pl.loop(start, stop)
        def _(j):
            cols = pl.ds(pl.multiple_of(j * 256, 256), 256)
            pg[:, cols] = dot(gv[:, 0:INTO], wv[cols, :], 1, 1)

    partial_input_grad(0, 3)
    forward(x_hop, 2, 0, 1)
    partial_input_grad(3, 6)
    forward(x_hop, 2, 2, 3)
    weights_to_plane()
    partial_input_grad(6, 9)
    forward(x_hop, 3, 0)

    for i in (6, 7):
        loads[i].wait()
    for b, (at, width) in enumerate(COLS):
        high, low = split(sw[0 if b == 0 else 1] if width == 256 else sn[b - 1])
        st[0:RANK, at:at + width] = high
        st[RANK:2 * RANK, at:at + width] = low
    loads[12].wait()
    for b, (at, width) in enumerate(COLS):
        t = dot(st[:, at:at + width], gv[:, at:at + width], 1, 1)
        high, low = split(t[:RANK] + t[RANK:])
        if b < 3:
            tx[b * RANK:(b + 1) * RANK, :] = high
            tx[96 + b * RANK:96 + (b + 1) * RANK, :] = low
        else:
            ty[0:RANK, :] = high
            ty[RANK:2 * RANK, :] = low
    qbd[...] = jnp.zeros_like(qbd)

    forward(x_hop, 3, 1)
    for i in (8, 9, 10, 11):
        loads[i].wait()

    def error_factors(start, stop):
        @pl.loop(start, stop)
        def _(j):
            rows = pl.ds(pl.multiple_of(j * 384, 384), 384)
            lanes = pl.ds(pl.multiple_of((j % 3) * 384, 384), 384)
            for b, (at, width) in enumerate(COLS):
                e = dot(st[:, at:at + width], ev[rows, at:at + width], 1, 1)
                fl[j // 3, b * RANK:(b + 1) * RANK, lanes] = e[:RANK] + e[RANK:]

    error_factors(0, 3)
    forward(x_hop, 3, 2)
    error_factors(3, 6)
    forward(x_hop, 3, 3)
    forward(x_hop, 4, 0, 1)
    first(y_hop)
    loads[13].wait()
    finish_ring(x_hop)

    @pl.loop(0, 6)
    def _(j):
        cols = pl.ds(pl.multiple_of(j * 384, 384), 384)
        lanes = pl.ds(pl.multiple_of((j % 3) * 384, 384), 384)
        f = dot(tx[...], xf[:, cols])
        fl[j // 3, 0:96, lanes] += f[:96] + f[96:]

    a_copy(0).start()

    def sums_into(start, stop):
        @pl.loop(start, stop)
        def _(j):
            rows = pl.ds(pl.multiple_of(j * 256, 256), 256)
            total = dot(xf[:, rows], gv[:, 0:INTO], 0, 0) + ev[rows, 0:INTO].astype(F32)
            high, low = split(total)
            sh[rows, 0:INTO] = high
            sl[rows, 0:INTO] = low

    forward(y_hop, 2, 0, 1, 2)
    forward(y_hop, 2, 3)
    weights_to_mate()
    sums_into(0, 3)
    to_reducers(0)
    forward(y_hop, 3, 0)
    sums_into(3, 6)
    forward(y_hop, 3, 1)
    sums_into(6, 9)
    forward(y_hop, 3, 2, 3)
    forward(y_hop, 4, 0, 1)
    from_reducers(0)
    add_neighbour_features()
    loads[14].wait()
    finish_ring(y_hop)
    z_first(1, 0)

    @pl.loop(0, 6)
    def _(j):
        cols = pl.ds(pl.multiple_of(j * 384, 384), 384)
        lanes = pl.ds(pl.multiple_of((j % 3) * 384, 384), 384)
        f = dot(ty[...], yf[:, cols])
        fl[j // 3, 96:128, lanes] += f[:RANK] + f[RANK:]

    a_copy(1).start()
    z_first(2, 1)
    to_mate(0)

    def gram_schmidt(block, which):
        @pl.loop(0, 8)
        def _(i):
            norms = {}
            kept = {}
            for b in which:
                row = [ff[h, pl.ds(b * RANK + block * 8 + i, 1), :] for h in (0, 1)]
                for h in (0, 1):
                    wide = jnp.broadcast_to(row[h], (8, HALF))
                    if len(which) == 1:
                        kept[h] = wide
                    else:
                        rowbuf[h, b * 8:b * 8 + 8, :] = wide
                norms[b] = jnp.sum(row[0] * row[0] + row[1] * row[1], axis=1, keepdims=True)
            def row_of(h, b):
                return kept[h] if kept else rowbuf[h, b * 8:b * 8 + 8, :]

            later = lax.broadcasted_iota(jnp.int32, (8, 1), 0) > i
            scales = {}
            for b in which:
                for t in range(block, 4):
                    at = slice(b * RANK + t * 8, b * RANK + t * 8 + 8)
                    dots = jnp.sum(
                        ff[0, at, :] * row_of(0, b) + ff[1, at, :] * row_of(1, b),
                        axis=1, keepdims=True,
                    )
                    scale = dots / norms[b]
                    scales[b, t] = jnp.where(later, scale, 0.0) if t == block else scale
            for b in which:
                for t in range(block, 4):
                    at = slice(b * RANK + t * 8, b * RANK + t * 8 + 8)
                    for h in (0, 1):
                        ff[h, at, :] -= scales[b, t] * row_of(h, b)

    def right_factors(which):
        for b in which:
            at = slice(b * RANK, (b + 1) * RANK)
            squares = jnp.sum(
                ff[0, at, :] * ff[0, at, :] + ff[1, at, :] * ff[1, at, :], axis=1, keepdims=True
            )
            size = jnp.sqrt(squares)
            for h in (0, 1):
                unit = ff[h, at, :] / size
                ff[h, at, :] = unit
                high, low = split(unit)
                pb[2 * b * RANK:(2 * b + 1) * RANK, h * HALF:(h + 1) * HALF] = high
                pb[(2 * b + 1) * RANK:(2 * b + 2) * RANK, h * HALF:(h + 1) * HALF] = low
        for b in which:
            at, width = COLS[b]
            both = dot(pb[2 * b * RANK:(2 * b + 2) * RANK, :], sh[:, at:at + width])
            rest = dot(pb[2 * b * RANK:(2 * b + 1) * RANK, :], sl[:, at:at + width])
            ql[:, at:at + width] = both[:RANK] + both[RANK:] + rest

    into = (0, 1, 2)
    outof = (3,)

    @pl.loop(0, 9)
    def _(j):
        rows = pl.ds(pl.multiple_of(j * 256, 256), 256)
        total = dot(yf[:, rows], gv[:, INTO:ALL], 0, 0) + ev[rows, INTO:ALL].astype(F32)
        high, low = split(total)
        sh[rows, INTO:ALL] = high
        sl[rows, INTO:ALL] = low

    z_step(2, 0)
    to_reducers(1)
    z_step(3, 1)
    from_mate(0)
    gram_schmidt(0, into)
    from_reducers(1)
    gram_schmidt(1, into)
    gram_schmidt(2, into)
    gram_schmidt(3, into)
    to_mate(1)
    right_factors(into)
    from_mate(1)
    gram_schmidt(0, outof)
    gram_schmidt(1, outof)
    z_step(3, 0)
    gram_schmidt(2, outof)
    gram_schmidt(3, outof)
    right_factors(outof)

    place = dp % 8
    line = dp // 8

    def part_of(j):
        return (
            pl.ds(pl.multiple_of((j % 4) * 8, 8), 8),
            pl.ds(pl.multiple_of((j // 4) * 384, 384), 384),
        )

    own_part = part_of(place)

    def e_copy(k):
        other = (place + k) % 8
        rows, lanes = part_of(other)
        return pltpu.make_async_remote_copy(
            src_ref=ql.at[rows, lanes], dst_ref=rq.at[k - 1],
            send_sem=e_send.at[k - 1], recv_sem=e_recv.at[k - 1],
            device_id=(line * 8 + other, mp), device_id_type=MESH,
        )

    def f_copy(k):
        return pltpu.make_async_remote_copy(
            src_ref=ry.at[line], dst_ref=ry.at[line],
            send_sem=f_send.at[k - 1], recv_sem=f_recv.at[k - 1],
            device_id=(((line + k) % 4) * 8 + place, mp), device_id_type=MESH,
        )

    def h_copy(k):
        own = qf.at[own_part[0], own_part[1]]
        return pltpu.make_async_remote_copy(
            src_ref=own, dst_ref=own,
            send_sem=h_send.at[k - 1], recv_sem=h_recv.at[k - 1],
            device_id=(line * 8 + (place + k) % 8, mp), device_id_type=MESH,
        )

    @pl.loop(1, 8)
    def _(k):
        e_copy(k).start()

    def left_by_rows(start, stop):
        @pl.loop(start, stop)
        def _(j):
            lanes = pl.ds(pl.multiple_of((j % 3) * 384, 384), 384)
            rows = pl.ds(pl.multiple_of(j * 384, 384), 384)
            by_row = jnp.transpose(ff[j // 3, :, lanes])
            pt[rows, :] = by_row
            high, low = split(by_row)
            pc[rows, 0:128] = high
            pc[rows, 128:256] = high
            pc[rows, 256:384] = low

    z_step(4, 1)
    left_by_rows(0, 2)

    @pl.loop(1, 8)
    def _(k):
        e_copy(k).wait_recv()

    ry[line] = ql[own_part[0], own_part[1]] + jnp.sum(rq[...], axis=0)

    @pl.loop(1, 4)
    def _(k):
        f_copy(k).start()

    left_by_rows(2, 4)

    @pl.loop(1, 4)
    def _(k):
        f_copy(k).wait_recv()

    qf[own_part[0], own_part[1]] = (ry[0] + ry[1] + ry[2] + ry[3]) * (1.0 / N_DP)

    @pl.loop(1, 8)
    def _(k):
        h_copy(k).start()

    z_step(4, 0)
    left_by_rows(4, 6)
    mine = jnp.transpose(pt[pl.ds(pl.multiple_of(dp * ROWS_P, 8), ROWS_P), :])
    for b, ref in enumerate((wide_p.at[0], narrow_p.at[0], narrow_p.at[1], wide_p.at[1])):
        ref[0] = mine[b * RANK:(b + 1) * RANK]

    @pl.loop(1, 8)
    def _(k):
        h_copy(k).wait_recv()

    for b, (at, width) in enumerate(COLS):
        q = qf[:, at:at + width]
        (wide_q, narrow_q)[width == 128][(0, 0, 1, 1)[b]] = q
        high, low = split(q)
        qbd[b * RANK:(b + 1) * RANK, at:at + width] = high
        qbd[128 + b * RANK:128 + (b + 1) * RANK, at:at + width] = low
        qbd[256 + b * RANK:256 + (b + 1) * RANK, at:at + width] = high

    @pl.loop(0, 9)
    def _(j):
        rows = pl.ds(pl.multiple_of(j * 256, 256), 256)
        low_rank = dot(pc[rows, :], qbd[...])
        new = (sh[rows, :].astype(F32) + sl[rows, :].astype(F32) - low_rank).astype(BF16)
        for b, ref in enumerate((wide_new, narrow_new, narrow_new, wide_new)):
            at, width = COLS[b]
            ref[0, (0, 0, 1, 1)[b], rows, :] = new[:, at:at + width]


    for way in (0, 1):
        for role in (0, 1):
            z_hop(way, 4, role)[0].wait_recv()
    own = pl.ds(pl.multiple_of(mp * SHARE, SHARE), SHARE)
    input_grad[...] = (pg[own, :] + rr[0, 3] + rr[1, 3]).astype(BF16)

    drain_neighbours()
    drain_ring(x_hop)
    drain_ring(y_hop)
    for way in (0, 1):
        for step in (1, 2, 3, 4):
            for role in (0, 1):
                if (step, role) != (1, 1):
                    z_hop(way, step, role)[0].wait_send()

    @pl.loop(1, 8)
    def _(k):
        e_copy(k).wait_send()
        h_copy(k).wait_send()

    @pl.loop(1, 4)
    def _(k):
        f_copy(k).wait_send()


def hand_out(*refs):
    sources, targets, sem = refs[:7], refs[7:14], refs[14]
    copies = [pltpu.make_async_copy(a, b, sem.at[i]) for i, (a, b) in enumerate(zip(sources, targets))]
    for copy in copies:
        copy.start()
    for copy in copies:
        copy.wait()


def on_device(*args):
    sems = pltpu.SemaphoreType.DMA
    vmem = pltpu.VMEM
    args = args[:9] + tuple(jnp.swapaxes(a, 1, 2) for a in args[9:])
    shapes = (
        ((SHARE, D), BF16),
        ((2, 1, RANK, ROWS_P), F32),
        ((2, 1, RANK, ROWS_P), F32),
        ((2, RANK, 256), F32),
        ((2, RANK, 128), F32),
        ((1, 2, D, 256), BF16),
        ((1, 2, D, 128), BF16),
    )
    outs = pl.pallas_call(
        kernel,
        out_shape=tuple(pltpu.VMEM(shape, dtype) for shape, dtype in shapes),
        in_specs=[pl.BlockSpec(memory_space=pltpu.HBM)] * 11,
        out_specs=tuple([pl.BlockSpec(memory_space=pltpu.VMEM)] * 7),
        scratch_shapes=[
            vmem((TOK, D), BF16),
            vmem((TOK, D), BF16),
            vmem((TOK, ALL), BF16),
            vmem((D, INTO), BF16),
            vmem((D, ALL), BF16),
            vmem((2, RANK, 256), F32),
            vmem((2, RANK, 128), F32),
            vmem((2 * RANK, ALL), BF16),
            vmem((192, TOK), BF16),
            vmem((64, TOK), BF16),
            vmem((TOK, D), F32),
            vmem((2, 4, SHARE, D), F32),
            vmem((D, ALL), BF16),
            vmem((D, ALL), BF16),
            vmem((2, NEAR, INTO), BF16),
            vmem((2, SHARE, INTO), BF16),
            vmem((2, 128, HALF), F32),
            vmem((128, HALF), F32),
            vmem((CHIPS - 1, 8, HALF), F32),
            vmem((CHIPS - 1, 8, 384), F32),
            vmem((2, 128, HALF), F32),
            vmem((2, 32, HALF), F32),
            vmem((256, D), BF16),
            vmem((D, 128), F32),
            vmem((D, 384), BF16),
            vmem((RANK, ALL), F32),
            vmem((7, 8, 384), F32),
            vmem((4, 8, 384), F32),
            vmem((RANK, ALL), F32),
            vmem((384, ALL), BF16),
            sems((15,)),
            sems((2, 4, 4)), sems((2, 4, 4)),
            sems((2, 4, 4)), sems((2, 4, 4)),
            sems((2, 4, 2)), sems((2, 4, 2)),
            sems((2, 3)), sems((2, 3)),
            sems((2, CHIPS - 1)), sems((2, CHIPS - 1)),
            sems((2,)), sems((2,)),
            sems((2,)), sems((2,)),
            sems((2, CHIPS - 1)), sems((2, CHIPS - 1)),
            sems((2, CHIPS - 1)), sems((2, CHIPS - 1)),
            sems((2,)), sems((2,)),
            sems((7,)), sems((7,)),
            sems((3,)), sems((3,)),
            sems((7,)), sems((7,)),
        ],
        compiler_params=pltpu.CompilerParams(
            collective_id=0, has_side_effects=True, vmem_limit_bytes=59 * 1024 * 1024
        ),
    )(*args)
    outs = pl.pallas_call(
        hand_out,
        out_shape=tuple(jax.ShapeDtypeStruct(shape, dtype) for shape, dtype in shapes),
        in_specs=[pl.BlockSpec(memory_space=pltpu.VMEM)] * 7,
        out_specs=tuple([pl.BlockSpec(memory_space=pl.ANY)] * 7),
        scratch_shapes=[sems((7,))],
        compiler_params=pltpu.CompilerParams(vmem_limit_bytes=16 * 1024 * 1024),
    )(*outs)
    turned = [jnp.swapaxes(a, -1, -2) for a in outs[1:5]]
    return (outs[0], *turned, *outs[5:])


def solution(mesh):
    return jax.shard_map(
        on_device,
        mesh=mesh,
        in_specs=(
            P(("dp", "mp"), None),
            P(("dp", "mp"), None),
            P("dp", "mp"),
            P("dp", "mp"),
            P(None, "dp", "mp"),
            P(None, "mp"),
            P(None, None, "mp"),
            P("dp", None, None, "mp"),
            P("dp", None, None, "mp"),
            P(None, "mp", None),
            P(None, "mp", None),
        ),
        out_specs=(
            P(("dp", "mp"), None),
            P(None, "mp", "dp", None),
            P(None, "mp", "dp", None),
            P(None, "mp", None),
            P(None, "mp", None),
            P("dp", None, None, "mp"),
            P("dp", None, None, "mp"),
        ),
        check_vma=False,
    )
```
